256 devices in a mesh: band: 4 (over x), dom: 64 (over z, y, core).
Axes of the slice: x: 4, y: 4, z: 8, core: 2. Of those that a mesh axis runs over, the one named last changes fastest.
Arguments:
- orbitals: bfloat16 [343, 1536, 512], P(None, 'dom', 'band'), may hold values from -6 to 6
- occupancy: float32 [512], P('band'), may hold values from 0 to 0.00390625
- shape_values: bfloat16 [512, 343], replicated, may hold values from -0.3125 to 0.3125
- shape_grads: bfloat16 [3, 512, 343], replicated, may hold values from -6 to 6
- cell_slot: int32 [1536], P('dom'), may hold values from 0 to 3071, as said below
- slot_cell: int32 [3072], P('dom'), may hold values from -1 to 1535, as said below
- potential_nodes: float32 [729, 3072], P(None, 'dom'), may hold values from -6 to 6
- stiffness: float32 [729, 729], replicated, may hold values from -0.21875 to 0.21875
- stiff_scale: float32 [3072], P('dom'), may hold values from 0.5 to 2
- electro_shape: float32 [512, 729], replicated, may hold values from -0.21875 to 0.21875
- core_density: float32 [3072, 512], P('dom'), may hold values from 0.1 to 1
- quad_weight: float32 [3072, 512], P('dom'), may hold values from 0.25 to 4
Outputs:
- hamiltonian_action: bfloat16 [343, 1536, 512], P(None, 'dom', 'band')
- poisson_residual: float32 [729, 3072], P(None, 'dom')
The draws below stay inside these ranges and needn't reach their ends.
Inputs may be any that keep to these rules, and one draw needn't show every extreme that they name: cell_slot is the owner domain times 48 plus the position in it, distinct over cells. The cells of one wavefunction domain go to exactly 12 electrostatics domains, 2 cells to each; an electrostatics domain holds 48 cells or none. slot_cell is the inverse of cell_slot: slot_cell[cell_slot[c]] = c, and -1 in every other slot.
All inputs are finite; a program needn't handle non-finite values.
Results may differ from the reference program's by a relative error of at most 0.0045.
Values sent between devices are 32-bit elements; how exact they have to be, the bound alone decides.
No kernel may reach another device: no remote copies, remote signals or barrier semaphores. Data moves between devices by JAX's collectives and lax.ppermute only.
A program may use at most 64 MiB of HBM per device.

```python
import math
import jax
import jax.numpy as jnp
from jax import lax

NW = 343
Q = 512
NE = 729
BANDS = 512
CELL_DEV = 24
GROUPS = 12
CAP = 2
ESLOT = 48
CELLS = 1536
SLOTS = 3072
N_DOM = 64


def owner_maps(key):
    cell_total = N_DOM * CELL_DEV
    key_dom, key_shift, key_cells, key_slots = jax.random.split(key, 4)
    middle = 1 + jax.random.permutation(key_dom, N_DOM - 2).astype(jnp.int32)
    relabel = jnp.concatenate([jnp.array([N_DOM - 1], jnp.int32), middle[:1], jnp.array([0], jnp.int32), middle[1:]])
    shifts = 2 * jax.random.permutation(key_shift, N_DOM // 2)[:GROUPS]
    orders = jax.vmap(lambda subkey: jax.random.permutation(subkey, CELL_DEV))(jax.random.split(key_cells, N_DOM))
    members = orders // CAP
    source = jnp.arange(N_DOM, dtype=jnp.int32)[:, None]
    position = (2 * (source // 2) + shifts[members]) % N_DOM
    owners = relabel[position].reshape(cell_total).astype(jnp.int32)
    onehot = (owners[:, None] == jnp.arange(N_DOM, dtype=jnp.int32)[None, :]).astype(jnp.int32)
    arrival = jnp.sum((jnp.cumsum(onehot, axis=0) - 1) * onehot, axis=1)
    places = jax.vmap(lambda subkey: jax.random.permutation(subkey, ESLOT))(jax.random.split(key_slots, N_DOM))
    cell_slot = (owners * ESLOT + places[owners, arrival]).astype(jnp.int32)
    slot_cell = jnp.full((N_DOM * ESLOT,), -1, jnp.int32).at[cell_slot].set(jnp.arange(cell_total, dtype=jnp.int32))
    return (cell_slot, slot_cell)


def draw_cell_slot(key, part):
    return owner_maps(key)[0]


def draw_slot_cell(key, part):
    return owner_maps(key)[1]


def block_levels(key, dims, cuts, smallest, top_value):
    factor_of = 1.0
    for dim, parts in cuts:
        steps = jax.random.uniform(jax.random.fold_in(jax.random.fold_in(key, 6), dim), (parts,), jnp.float32, smallest / len(cuts), top_value / len(cuts))
        factor_of = factor_of * jnp.repeat(jnp.exp(steps), dims[dim] // parts).reshape((-1,) + (1,) * (len(dims) - 1 - dim))
    return factor_of


def scatter_about(stream_key, shape, scale, limit, cuts=(), kind=jnp.bfloat16):
    drawn = scale * jax.random.normal(stream_key, shape, jnp.float32)
    if cuts:
        drawn = drawn * block_levels(stream_key, shape, cuts, -0.22, 0.18)
    return jnp.clip(drawn, -limit, limit).astype(kind)


def setup_inputs(seed: int = 0) -> dict:
    splits = jax.random.split(jax.random.key(seed), 13)
    orbitals = scatter_about(splits[0], (NW, CELLS, BANDS), 1.0, 6.0, ((1, 64), (2, 4)))
    occupancy = jnp.clip(0.00390625 * jax.random.uniform(splits[1], (BANDS,), jnp.float32) ** block_levels(splits[1], (BANDS,), ((0, 4),), -0.2, 0.2), 0.0, 0.00390625)
    shape_values = scatter_about(splits[2], (Q, NW), NW ** -0.5, 0.3125)
    shape_grads = scatter_about(splits[3], (3, Q, NW), 2.3, 6.0)
    cell_slot = draw_cell_slot(jax.random.fold_in(splits[12], 71), 0)
    slot_cell = draw_slot_cell(jax.random.fold_in(splits[12], 71), 0)
    potential_nodes = scatter_about(splits[6], (NE, SLOTS), 1.0, 6.0, ((1, 64),), jnp.float32)
    stiffness = scatter_about(splits[7], (NE, NE), NE ** -0.5, 0.21875, (), jnp.float32)
    stiff_scale = jnp.clip(jnp.exp(math.log(2.0) - 1.3862944 * jax.random.uniform(splits[8], (SLOTS,), jnp.float32) ** block_levels(splits[8], (SLOTS,), ((0, 64),), -0.2, 0.2)), 0.5, 2.0)
    electro_shape = scatter_about(splits[9], (Q, NE), NE ** -0.5, 0.21875, (), jnp.float32)
    core_density = jnp.clip(jnp.exp(math.log(1.0) - 2.3025851 * jax.random.uniform(splits[10], (SLOTS, Q), jnp.float32) ** block_levels(splits[10], (SLOTS, Q), ((0, 64),), -0.2, 0.2)), 0.1, 1.0)
    quad_weight = jnp.clip(jnp.exp(math.log(4.0) - 2.7725887 * jax.random.uniform(splits[11], (SLOTS, Q), jnp.float32) ** block_levels(splits[11], (SLOTS, Q), ((0, 64),), -0.2, 0.2)), 0.25, 4.0)
    return {"orbitals": orbitals, "occupancy": occupancy, "shape_values": shape_values, "shape_grads": shape_grads, "cell_slot": cell_slot, "slot_cell": slot_cell, "potential_nodes": potential_nodes, "stiffness": stiffness, "stiff_scale": stiff_scale, "electro_shape": electro_shape, "core_density": core_density, "quad_weight": quad_weight}


slater_coef = 0.7385587663820224
bound_kappa = 0.804
slope_coef = 0.2195149727645171
reduced_coef = 0.026121172985233605

def exchange_energy(density, square):
    power_four = density * jnp.cbrt(density)
    reduced = reduced_coef * square / (power_four * power_four)
    enhance = 1.0 + bound_kappa - bound_kappa / (1.0 + slope_coef * reduced / bound_kappa)
    return -slater_coef * power_four * enhance

def exchange_parts(density, square):
    return jax.grad(lambda dens_in, square_in: jnp.sum(exchange_energy(dens_in, square_in)), argnums=(0, 1))(density, square)

def weighted_potential(density, gradient, weight, hartree):
    square = lax.optimization_barrier(jnp.sum(gradient * gradient, axis=0))
    d_density, d_square = exchange_parts(density, square)
    first_term = weight * (d_density + hartree)
    other_terms = 2.0 * weight * d_square * gradient
    return jnp.concatenate([first_term[None], other_terms], axis=0)

def poisson_apply(density, weight, node_field, cell_scale, stiffness, interp):
    stiff_part = jnp.dot(stiffness, node_field, precision=lax.Precision.HIGHEST)
    load_term = jnp.dot(interp.T, weight * density, precision=lax.Precision.HIGHEST)
    return cell_scale * stiff_part - load_term

def quad_terms(shape_table, orbit_block):
    node_count, cell_count, band_count = orbit_block.shape
    flattened = jnp.dot(shape_table, orbit_block.reshape(node_count, cell_count * band_count), preferred_element_type=jnp.float32)
    return flattened.reshape(4, -1, cell_count, band_count)

def density_terms(quad_vals, occupancy):
    weighted_lead = quad_vals[0] * occupancy
    first_term = lax.optimization_barrier(jnp.sum(weighted_lead * quad_vals[0], axis=-1))
    other_terms = 2.0 * lax.optimization_barrier(jnp.sum(weighted_lead[None] * quad_vals[1:], axis=-1))
    return jnp.concatenate([first_term[None], other_terms], axis=0)

def apply_potential(shape_table, quad_vals, weighted):
    expanded = weighted[..., None]
    value_term = expanded[0] * quad_vals[0] + (expanded[1] * quad_vals[1] + expanded[2] * quad_vals[2] + expanded[3] * quad_vals[3])
    grad_terms = expanded[1:] * quad_vals[0][None]
    products = jnp.concatenate([value_term[None], grad_terms], axis=0).astype(jnp.bfloat16)
    products = lax.optimization_barrier(products).astype(jnp.float32)
    node_count = shape_table.shape[1]
    cell_count, band_count = (quad_vals.shape[2], quad_vals.shape[3])
    result = jnp.dot(shape_table.T, products.reshape(-1, cell_count * band_count), preferred_element_type=jnp.float32)
    return result.astype(jnp.bfloat16).reshape(node_count, cell_count, band_count)

def reference(orbitals, occupancy, shape_values, shape_grads, cell_slot, slot_cell, potential_nodes, stiffness, stiff_scale, electro_shape, core_density, quad_weight):
    core_field = core_density.T
    weight_field = quad_weight.T
    shape_table = jnp.concatenate([shape_values[None], shape_grads], axis=0).reshape(4 * Q, NW).astype(jnp.float32)

    def first_pass(block_index):
        orbit_block = lax.dynamic_slice_in_dim(orbitals, block_index * CELL_DEV, CELL_DEV, 1).astype(jnp.float32)
        return density_terms(quad_terms(shape_table, orbit_block), occupancy)
    partial_value = lax.map(first_pass, jnp.arange(N_DOM, dtype=jnp.int32))
    partial_value = partial_value.transpose(1, 2, 0, 3).reshape(4, Q, CELLS)
    filled = slot_cell >= 0
    gathered = jnp.take(partial_value, jnp.maximum(slot_cell, 0), axis=2)
    arrived = jnp.where(filled[None, None, :], gathered, jnp.float32(0.0))
    density = core_field + arrived[0]
    hartree = jnp.dot(electro_shape, potential_nodes, precision=lax.Precision.HIGHEST)
    weighted = weighted_potential(density, arrived[1:], weight_field, hartree)
    residual = poisson_apply(density, weight_field, potential_nodes, stiff_scale, stiffness, electro_shape)
    returned = jnp.take(weighted, cell_slot, axis=2)

    def second_pass(block_index):
        orbit_block = lax.dynamic_slice_in_dim(orbitals, block_index * CELL_DEV, CELL_DEV, 1).astype(jnp.float32)
        quad_vals = quad_terms(shape_table, orbit_block)
        block_pot = lax.dynamic_slice_in_dim(returned, block_index * CELL_DEV, CELL_DEV, 2)
        return apply_potential(shape_table, quad_vals, block_pot)
    action = lax.map(second_pass, jnp.arange(N_DOM, dtype=jnp.int32))
    action = action.transpose(1, 0, 2, 3).reshape(NW, CELLS, BANDS)
    return (action, residual)
```

```python
import functools

import jax
import jax.numpy as jnp
from jax import lax
from jax.experimental import pallas as pl
from jax.experimental.pallas import tpu as pltpu
from jax.sharding import PartitionSpec as P

F32, BF16, I32 = jnp.float32, jnp.bfloat16, jnp.int32
NODES, CELLS, BANDS, POINTS = 343, 24, 128, 512
KPAD = 384
SLOTS, ENODES, DOMAINS, CAP = 48, 729, 64, 2
ROWS = DOMAINS * CAP
RANKS, PART = 4, 128
GROUP = 4
STEP = 49
HIGHEST = lax.Precision.HIGHEST
NT = (((1,), (1,)), ((), ()))
MIB = 1 << 20

slater_coef = 0.7385587663820224
bound_kappa = 0.804
slope_coef = 0.2195149727645171
reduced_coef = 0.026121172985233605

VM = pl.BlockSpec(memory_space=pltpu.VMEM)
SM = pl.BlockSpec(memory_space=pltpu.SMEM)
HB = pl.BlockSpec(memory_space=pl.ANY)


def params(mib):
    return pltpu.CompilerParams(vmem_limit_bytes=mib * MIB)


def cost(flops, nbytes):
    return pl.CostEstimate(flops=int(flops), bytes_accessed=int(nbytes), transcendentals=0)


def lanes(index):
    return slice(index * 128, index * 128 + 128)


def fields_kernel(
    band_ref, slot_cell_ref, cell_slot_ref, nodes_ref, shape_ref, core_ref, weight_ref,
    send_ref, wave_row_ref, slot_row_ref, field_ref, count_ref,
):
    del band_ref

    def clear(d, carry):
        count_ref[d] = 0
        return carry

    lax.fori_loop(0, DOMAINS, clear, 0)
    field_ref[:, lanes(0)] = core_ref[...]
    field_ref[:, lanes(1)] = weight_ref[...]
    field_ref[:, lanes(2)] = jnp.dot(
        nodes_ref[...], shape_ref[...], precision=HIGHEST, preferred_element_type=F32
    )
    for s in range(SLOTS):
        cell = slot_cell_ref[s]
        slot_row_ref[s] = -1

        @pl.when(cell >= 0)
        def _():
            source = lax.shift_right_logical(cell * 10923, 18)
            place = count_ref[source]
            count_ref[source] = place + 1
            row = source * CAP + jnp.minimum(place, CAP - 1)
            slot_row_ref[s] = row
            send_ref[row] = field_ref[s : s + 1, :]

    def forget(d, carry):
        count_ref[d] = -1
        return carry

    lax.fori_loop(0, DOMAINS, forget, 0)

    def place_cell(c, carry):
        slot = cell_slot_ref[c]
        owner = lax.shift_right_logical(slot * 21846, 20)
        other = count_ref[owner]
        known = other >= 0
        first = jnp.maximum(other, 0)
        later = cell_slot_ref[first] > slot
        wave_row_ref[c] = owner * CAP + jnp.where(known & jnp.logical_not(later), 1, 0)

        @pl.when(known & later)
        def _():
            wave_row_ref[first] = owner * CAP + 1

        count_ref[owner] = c
        return carry

    lax.fori_loop(0, CELLS, place_cell, 0)


def pack_fields(band, slot_cell, cell_slot, nodes, shape, core, weight):
    quarter = lambda i, b: (0, b[0])
    return pl.pallas_call(
        fields_kernel,
        out_shape=(
            jax.ShapeDtypeStruct((ROWS, 1, 3 * PART), F32),
            jax.ShapeDtypeStruct((CELLS,), I32),
            jax.ShapeDtypeStruct((SLOTS,), I32),
        ),
        grid_spec=pltpu.PrefetchScalarGridSpec(
            num_scalar_prefetch=1,
            grid=(1,),
            in_specs=[
                SM,
                SM,
                pl.BlockSpec((SLOTS, ENODES), lambda i, b: (0, 0)),
                pl.BlockSpec((ENODES, PART), quarter),
                pl.BlockSpec((SLOTS, PART), quarter),
                pl.BlockSpec((SLOTS, PART), quarter),
            ],
            out_specs=(pl.BlockSpec((ROWS, 1, 3 * PART), lambda i, b: (0, 0, 0)), SM, SM),
            scratch_shapes=[pltpu.VMEM((SLOTS, 3 * PART), F32), pltpu.SMEM((DOMAINS,), I32)],
        ),
        compiler_params=params(8),
        cost_estimate=cost(12 * SLOTS * ENODES * PART, 2 * MIB),
        name="pack_fields",
    )(band, slot_cell, cell_slot, nodes, shape, core, weight)


def first_kernel(
    orb_ref, occ_ref, val_ref, grad_ref, part_ref, quad_ref,
    wide_ref, node_ref, table_ref, spread_ref, slab_ref, sem_ref,
):
    table_ref[:, NODES - 7 :, :] = jnp.zeros((4, KPAD - NODES + 7, POINTS), BF16)
    table_ref[0, :NODES, :] = val_ref[...]
    for k in range(3):
        table_ref[k + 1, :NODES, :] = grad_ref[k]
    spread_ref[...] = jnp.broadcast_to(occ_ref[...], (BANDS, BANDS)).T

    def widen(i, carry):
        part = orb_ref[pl.ds(i * STEP, STEP)].astype(F32)
        wide_ref[pl.ds(i * STEP * CELLS, STEP * CELLS), :] = part.reshape(STEP * CELLS, BANDS)
        return carry

    lax.fori_loop(0, NODES // STEP, widen, 0)
    wide_ref[NODES * CELLS :, :] = jnp.zeros(((KPAD - NODES) * CELLS, BANDS), F32)

    def send(g):
        return pltpu.make_async_copy(
            slab_ref.at[g % 2], quad_ref.at[pl.ds(g * GROUP, GROUP)], sem_ref.at[g % 2]
        )

    for g in range(CELLS // GROUP):
        slab = slab_ref.at[g % 2]
        if g >= 2:
            send(g - 2).wait()
        for i in range(GROUP):
            block = wide_ref[pl.ds(g * GROUP + i, KPAD, stride=CELLS), :]
            node_ref[i * BANDS : (i + 1) * BANDS, :] = block.T.astype(BF16)
        for k in range(4):
            values = jnp.dot(node_ref[...], table_ref[k], preferred_element_type=F32)
            for i in range(GROUP):
                slab[i, k] = values[i * BANDS : (i + 1) * BANDS]
        for i in range(GROUP):
            c = g * GROUP + i
            for lane in range(POINTS // 128):
                cols = lanes(lane)
                lead = slab[i, 0, :, cols]
                scaled = spread_ref[...] * lead
                part_ref[0, c : c + 1, cols] = jnp.sum(scaled * lead, axis=0, keepdims=True)
                for k in range(1, 4):
                    term = slab[i, k, :, cols]
                    part_ref[k, c : c + 1, cols] = 2.0 * jnp.sum(scaled * term, axis=0, keepdims=True)
        send(g).start()
    send(CELLS // GROUP - 2).wait()
    send(CELLS // GROUP - 1).wait()


def first_pass(orbitals, occupancy, values, grads):
    return pl.pallas_call(
        first_kernel,
        out_shape=(
            jax.ShapeDtypeStruct((4, CELLS, POINTS), F32),
            jax.ShapeDtypeStruct((CELLS, 4, BANDS, POINTS), F32),
        ),
        in_specs=[VM] * 4,
        out_specs=(VM, HB),
        scratch_shapes=[
            pltpu.VMEM((KPAD * CELLS, BANDS), F32),
            pltpu.VMEM((GROUP * BANDS, KPAD), BF16),
            pltpu.VMEM((4, KPAD, POINTS), BF16),
            pltpu.VMEM((BANDS, BANDS), F32),
            pltpu.VMEM((2, GROUP, 4, BANDS, POINTS), F32),
            pltpu.SemaphoreType.DMA((2,)),
        ],
        compiler_params=params(32),
        cost_estimate=cost(2 * 2048 * 512 * 3072, 28 * MIB),
        name="first_pass",
    )(orbitals, occupancy, values, grads)


def density_kernel(row_ref, a_ref, b_ref, c_ref, d_ref, send_ref, sum_ref):
    sum_ref[...] = (a_ref[0] + b_ref[0]) + (c_ref[0] + d_ref[0])
    for c in range(CELLS):
        send_ref[row_ref[c]] = sum_ref[c : c + 1, :]


def pack_density(rows, parts):
    lead = pl.BlockSpec((1, CELLS, POINTS), lambda i: (0, 0, 0))
    return pl.pallas_call(
        density_kernel,
        out_shape=jax.ShapeDtypeStruct((ROWS, 1, POINTS), F32),
        grid=(1,),
        in_specs=[SM] + [lead] * 4,
        out_specs=pl.BlockSpec((ROWS, 1, POINTS), lambda i: (0, 0, 0)),
        scratch_shapes=[pltpu.VMEM((CELLS, POINTS), F32)],
        compiler_params=params(8),
        cost_estimate=cost(1e5, MIB // 2),
        name="pack_density",
    )(rows, *parts)


def exchange_terms(density, square):
    third = jnp.exp(jnp.log(density) * (1.0 / 3.0))
    power_four = density * third
    reduced = reduced_coef * square / (power_four * power_four)
    inner = 1.0 + slope_coef * reduced / bound_kappa
    slope = slope_coef / (inner * inner)
    enhance = 1.0 + bound_kappa - bound_kappa / inner
    d_density = -slater_coef * third * ((4.0 / 3.0) * enhance - (8.0 / 3.0) * reduced * slope)
    d_square = -slater_coef * reduced_coef * slope / power_four
    return d_density, d_square


def second_kernel(
    band_ref, row_ref, e0_ref, e1_ref, e2_ref, e3_ref, a_ref, b_ref, c_ref, d_ref,
    val_ref, grad_ref, quad_ref, out_ref,
    field_ref, wt_ref, wide_ref, table_ref, prod_ref, slab_ref, sem_ref,
):
    pairs = CELLS // 2

    def fetch(p):
        return pltpu.make_async_copy(
            quad_ref.at[pl.ds(2 * p, 2)], slab_ref.at[p % 3], sem_ref.at[p % 3]
        )

    fetch(0).start()
    fetch(1).start()
    table_ref[:, :POINTS] = val_ref[...]
    for k in range(3):
        table_ref[:, (k + 1) * POINTS : (k + 2) * POINTS] = grad_ref[k]
    for d, source in enumerate((e0_ref, e1_ref, e2_ref, e3_ref)):
        rank = (band_ref[0] + RANKS - d) & (RANKS - 1)
        for c in range(CELLS):
            row = row_ref[c]
            for f in range(3):
                field_ref[rank, f, c : c + 1, :] = source[row, :, lanes(f)]
    for q in range(RANKS):
        cols = lanes(q)
        total = [(a_ref[k, :, cols] + b_ref[k, :, cols]) + (c_ref[k, :, cols] + d_ref[k, :, cols]) for k in range(4)]
        core, weight, hartree = field_ref[q, 0], field_ref[q, 1], field_ref[q, 2]
        square = total[1] * total[1] + total[2] * total[2] + total[3] * total[3]
        d_density, d_square = exchange_terms(core + total[0], square)
        wt_ref[0, :, cols] = weight * (d_density + hartree)
        for k in range(1, 4):
            wt_ref[k, :, cols] = 2.0 * weight * d_square * total[k]

    def products(p):
        slab, prod = slab_ref.at[p % 3], prod_ref.at[p % 2]
        for half in range(2):
            c = 2 * p + half
            rows = slice(half * BANDS, half * BANDS + BANDS)
            for lane in range(POINTS // 128):
                cols = lanes(lane)
                r = [wt_ref[k, c : c + 1, cols] for k in range(4)]
                q = [slab[half, k, :, cols] for k in range(4)]
                value = r[0] * q[0] + (r[1] * q[1] + r[2] * q[2] + r[3] * q[3])
                prod[rows, cols] = value.astype(BF16)
                for k in range(1, 4):
                    prod[rows, lanes(4 * k + lane)] = (r[k] * q[0]).astype(BF16)

    def multiply(p):
        result = lax.dot_general(table_ref[...], prod_ref[p % 2], NT, preferred_element_type=F32)
        for half in range(2):
            wide_ref[pl.ds(2 * p + half, NODES, stride=CELLS), :] = result[:, half * BANDS : half * BANDS + BANDS]

    fetch(0).wait()
    products(0)
    for p in range(pairs):
        if p + 2 < pairs:
            fetch(p + 2).start()
        if p + 1 < pairs:
            fetch(p + 1).wait()
            products(p + 1)
        multiply(p)

    def narrow(i, carry):
        part = wide_ref[pl.ds(i * STEP * CELLS, STEP * CELLS), :].reshape(STEP, CELLS, BANDS)
        out_ref[pl.ds(i * STEP, STEP)] = part.astype(BF16)
        return carry

    lax.fori_loop(0, NODES // STEP, narrow, 0)


def second_pass(band, rows, fields, parts, values, grads, quads):
    return pl.pallas_call(
        second_kernel,
        out_shape=jax.ShapeDtypeStruct((NODES, CELLS, BANDS), BF16),
        in_specs=[SM, SM] + [VM] * 10 + [HB],
        out_specs=VM,
        scratch_shapes=[
            pltpu.VMEM((RANKS, 3, CELLS, PART), F32),
            pltpu.VMEM((4, CELLS, POINTS), F32),
            pltpu.VMEM((NODES * CELLS, BANDS), F32),
            pltpu.VMEM((NODES, 4 * POINTS), BF16),
            pltpu.VMEM((2, 2 * BANDS, 4 * POINTS), BF16),
            pltpu.VMEM((3, 2, 4, BANDS, POINTS), F32),
            pltpu.SemaphoreType.DMA((3,)),
        ],
        compiler_params=params(32),
        cost_estimate=cost(2 * 2048 * 343 * 3072, 30 * MIB),
        name="second_pass",
    )(band, rows, *fields, *parts, values, grads, quads)


def stiff_kernel(nodes_ref, stiff_ref, scale_ref, out_ref):
    product = lax.dot_general(nodes_ref[...], stiff_ref[...], NT, precision=HIGHEST, preferred_element_type=F32)
    spread = jnp.broadcast_to(scale_ref[...], (128, SLOTS)).T
    for j in range(0, ENODES, 128):
        width = min(128, ENODES - j)
        out_ref[:, j : j + width] = product[:, j : j + width] * spread[:, :width]


def stiff_part(nodes, stiffness, scale):
    return pl.pallas_call(
        stiff_kernel,
        out_shape=jax.ShapeDtypeStruct((SLOTS, ENODES), F32),
        in_specs=[VM] * 3,
        out_specs=VM,
        compiler_params=params(12),
        cost_estimate=cost(12 * SLOTS * ENODES * ENODES, 3 * MIB),
        name="stiff_part",
    )(nodes, stiffness, scale)


def residual_kernel(row_ref, arrived_ref, core_ref, weight_ref, shape_ref, stiff_ref, out_ref, dens_ref):
    for s in range(SLOTS):
        row = row_ref[s]
        value = arrived_ref[jnp.maximum(row, 0)]
        dens_ref[s : s + 1, :] = jnp.where(row >= 0, value, 0.0)
    source = weight_ref[...] * (core_ref[...] + dens_ref[...])
    load = lax.dot_general(source, shape_ref[...], NT, precision=HIGHEST, preferred_element_type=F32)
    out_ref[...] = stiff_ref[...] - load


def residual(rows, arrived, core, weight, shape, stiff):
    return pl.pallas_call(
        residual_kernel,
        out_shape=jax.ShapeDtypeStruct((SLOTS, ENODES), F32),
        in_specs=[SM] + [VM] * 5,
        out_specs=VM,
        scratch_shapes=[pltpu.VMEM((SLOTS, POINTS), F32)],
        compiler_params=params(12),
        cost_estimate=cost(12 * SLOTS * ENODES * POINTS, 3 * MIB),
        name="residual",
    )(rows, arrived, core, weight, shape, stiff)


def around_band(array, distance):
    return lax.ppermute(array, "band", [(i, (i + distance) % RANKS) for i in range(RANKS)])


def body(
    orbitals, occupancy, shape_values, shape_grads, cell_slot, slot_cell, potential_nodes,
    stiffness, stiff_scale, electro_shape, core_density, quad_weight,
):
    values, grads = shape_values.T, shape_grads.transpose(0, 2, 1)
    nodes, shape = potential_nodes.T, electro_shape.T
    band = lax.axis_index("band").astype(I32).reshape(1)

    send, wave_rows, slot_rows = pack_fields(band, slot_cell, cell_slot, nodes, shape, core_density, quad_weight)
    came = lax.all_to_all(send, "dom", split_axis=0, concat_axis=0, tiled=True)

    part, quads = first_pass(orbitals, occupancy.reshape(1, BANDS), values, grads)
    parts = [part] + [around_band(part, d) for d in (1, 2, 3)]

    stiff = stiff_part(nodes, stiffness, stiff_scale.reshape(1, SLOTS))

    fields = [came] + [around_band(came, d) for d in (1, 2, 3)]
    arrived = lax.all_to_all(pack_density(wave_rows, parts), "dom", split_axis=0, concat_axis=0, tiled=True)

    action = second_pass(band, wave_rows, fields, parts, values, grads, quads)
    rest = residual(slot_rows, arrived, core_density, quad_weight, shape, stiff)
    return action, rest.T


def solution(mesh):
    return jax.shard_map(
        body,
        mesh=mesh,
        in_specs=(
            P(None, "dom", "band"), P("band"), P(), P(), P("dom"), P("dom"),
            P(None, "dom"), P(), P("dom"), P(), P("dom", None), P("dom", None),
        ),
        out_specs=(P(None, "dom", "band"), P(None, "dom")),
        check_vma=False,
    )
```

```python
import functools

import jax
import jax.numpy as jnp
from jax import lax
from jax.experimental import pallas as pl
from jax.experimental.pallas import tpu as pltpu
from jax.sharding import PartitionSpec as P

F32, BF16, I32 = jnp.float32, jnp.bfloat16, jnp.int32
NODES, CELLS, BANDS, POINTS = 343, 24, 128, 512
KPAD = 384
SLOTS, ENODES, DOMAINS, CAP = 48, 729, 64, 2
ROWS = DOMAINS * CAP
RANKS, PART = 4, 128
GROUP = 4
STEP = 49
FIELDS = 3 * PART
WIDTH = FIELDS + POINTS
TERMS = 4 * CELLS
MIX = TERMS + RANKS * SLOTS
HIGHEST = lax.Precision.HIGHEST
NT = (((1,), (1,)), ((), ()))
MIB = 1 << 20

slater_coef = 0.7385587663820224
bound_kappa = 0.804
slope_coef = 0.2195149727645171
reduced_coef = 0.026121172985233605

VM = pl.BlockSpec(memory_space=pltpu.VMEM)
SM = pl.BlockSpec(memory_space=pltpu.SMEM)
HB = pl.BlockSpec(memory_space=pltpu.HBM)


def params(mib):
    return pltpu.CompilerParams(vmem_limit_bytes=mib * MIB)


def cost(flops, nbytes):
    return pl.CostEstimate(flops=int(flops), bytes_accessed=int(nbytes), transcendentals=0)


def lanes(index):
    return slice(index * 128, index * 128 + 128)


def first_kernel(
    band_ref, slot_cell_ref, cell_slot_ref,
    orb_hbm, occ_ref, val_hbm, nodes_hbm, shape_hbm, core_hbm, weight_hbm,
    send_hbm, node_hbm, wave_row_ref, slot_row_ref,
    orb_ref, val_ref, nodes_ref, shape_ref, field_ref, send_ref,
    wide_ref, node_ref, table_ref, spread_ref, sum_ref, count_ref, in_sem, orb_sem, out_sem, send_sem,
):
    mine = pl.ds(pl.multiple_of(band_ref[0] * PART, PART), PART)
    chunks = NODES // STEP

    def take(i):
        part = pl.ds(i * STEP, STEP)
        return pltpu.make_async_copy(orb_hbm.at[part], orb_ref.at[part], orb_sem.at[i])

    loads = [
        pltpu.make_async_copy(val_hbm, val_ref, in_sem.at[0]),
        pltpu.make_async_copy(nodes_hbm, nodes_ref, in_sem.at[1]),
        pltpu.make_async_copy(shape_hbm.at[:, mine], shape_ref, in_sem.at[2]),
        pltpu.make_async_copy(core_hbm.at[:, mine], field_ref.at[:, lanes(0)], in_sem.at[3]),
        pltpu.make_async_copy(weight_hbm.at[:, mine], field_ref.at[:, lanes(1)], in_sem.at[4]),
    ]
    for load in loads:
        load.start()
    for i in range(chunks):
        take(i).start()

    for d in range(DOMAINS + 1):
        count_ref[d] = 0
    for s in range(SLOTS):
        cell = slot_cell_ref[s]
        filled = cell >= 0
        source = jnp.where(filled, lax.shift_right_logical(cell * 10923, 18), DOMAINS)
        place = jnp.minimum(count_ref[source], CAP - 1)
        count_ref[source] = jnp.where(filled, place + 1, 0)
        slot_row_ref[s] = jnp.where(filled, source * CAP + place, ROWS)
    for d in range(DOMAINS):
        count_ref[d] = -1
    for c in range(CELLS):
        slot = cell_slot_ref[c]
        owner = lax.shift_right_logical(slot * 21846, 20)
        other = count_ref[owner]
        known = other >= 0
        first = jnp.maximum(other, 0)
        later = known & (cell_slot_ref[first] > slot)
        wave_row_ref[c] = owner * CAP + jnp.where(known & jnp.logical_not(later), 1, 0)
        target = jnp.where(later, first, c)
        wave_row_ref[target] = jnp.where(later, owner * CAP + 1, wave_row_ref[c])
        count_ref[owner] = c

    spread_ref[...] = jnp.broadcast_to(occ_ref[...], (BANDS, BANDS)).T
    table_ref[NODES - 7 :, :] = jnp.zeros((KPAD - NODES + 7, POINTS), BF16)
    wide_ref[NODES * CELLS :, :] = jnp.zeros(((KPAD - NODES) * CELLS, BANDS), F32)

    for load in loads:
        load.wait()
    table_ref[:NODES, :] = val_ref[...]
    field_ref[:, lanes(2)] = jnp.dot(
        nodes_ref[...], shape_ref[...], precision=HIGHEST, preferred_element_type=F32
    )
    for s in range(SLOTS):
        send_ref[slot_row_ref[s], :, :FIELDS] = field_ref[s : s + 1, :]

    for i in range(chunks):
        take(i).wait()
        part = orb_ref[pl.ds(i * STEP, STEP)].astype(F32)
        wide_ref[pl.ds(i * STEP * CELLS, STEP * CELLS), :] = part.reshape(STEP * CELLS, BANDS)

    def store(g):
        rows = pl.ds(g * GROUP * BANDS, GROUP * BANDS)
        return pltpu.make_async_copy(node_ref.at[rows], node_hbm.at[rows], out_sem.at[g])

    groups = CELLS // GROUP
    for g in range(groups):
        rows = slice(g * GROUP * BANDS, (g + 1) * GROUP * BANDS)
        for i in range(GROUP):
            c = g * GROUP + i
            block = wide_ref[pl.ds(c, KPAD, stride=CELLS), :]
            node_ref[c * BANDS : (c + 1) * BANDS, :] = block.T.astype(BF16)
        store(g).start()
        values = jnp.dot(node_ref[rows, :], table_ref[...], preferred_element_type=F32)
        for i in range(GROUP):
            c = g * GROUP + i
            for q in range(RANKS):
                lead = values[i * BANDS : (i + 1) * BANDS, lanes(q)]
                sum_ref[c : c + 1, lanes(q)] = jnp.sum(spread_ref[...] * lead * lead, axis=0, keepdims=True)
    for c in range(CELLS):
        send_ref[wave_row_ref[c], :, FIELDS:] = sum_ref[c : c + 1, :]
    leave = pltpu.make_async_copy(send_ref.at[pl.ds(0, ROWS)], send_hbm, send_sem)
    leave.start()
    for g in range(groups):
        store(g).wait()
    leave.wait()


def first_pass(band, slot_cell, cell_slot, orbitals, occupancy, values, nodes, shape, core, weight):
    return pl.pallas_call(
        first_kernel,
        out_shape=(
            jax.ShapeDtypeStruct((ROWS, 1, WIDTH), F32),
            jax.ShapeDtypeStruct((CELLS * BANDS, KPAD), BF16),
            jax.ShapeDtypeStruct((CELLS,), I32),
            jax.ShapeDtypeStruct((SLOTS,), I32),
        ),
        in_specs=[SM, SM, SM, HB, VM] + [HB] * 5,
        out_specs=(HB, HB, SM, SM),
        scratch_shapes=[
            pltpu.VMEM((NODES, CELLS, BANDS), BF16),
            pltpu.VMEM((NODES, POINTS), BF16),
            pltpu.VMEM((SLOTS, ENODES), F32),
            pltpu.VMEM((ENODES, PART), F32),
            pltpu.VMEM((SLOTS, FIELDS), F32),
            pltpu.VMEM((ROWS + 1, 1, WIDTH), F32),
            pltpu.VMEM((KPAD * CELLS, BANDS), F32),
            pltpu.VMEM((CELLS * BANDS, KPAD), BF16),
            pltpu.VMEM((KPAD, POINTS), BF16),
            pltpu.VMEM((BANDS, BANDS), F32),
            pltpu.VMEM((CELLS, POINTS), F32),
            pltpu.SMEM((DOMAINS + 1,), I32),
            pltpu.SemaphoreType.DMA((5,)),
            pltpu.SemaphoreType.DMA((NODES // STEP,)),
            pltpu.SemaphoreType.DMA((CELLS // GROUP,)),
            pltpu.SemaphoreType.DMA,
        ],
        compiler_params=params(60),
        cost_estimate=cost(2 * 512 * 512 * 3072, 8 * MIB),
        name="first_pass",
    )(band, slot_cell, cell_slot, orbitals, occupancy, values, nodes, shape, core, weight)


def gradient_kernel(
    band_ref, occ_ref, val_hbm, grad_hbm, node_hbm,
    part0_ref, part1_ref, part2_ref, part3_ref, table_hbm,
    val_ref, grad_ref, node_ref, table_ref, spread_ref, slab_ref, sum_ref, in_sem, node_sem, out_sem,
):
    groups = CELLS // GROUP

    def take(g):
        rows = pl.ds(g * GROUP * BANDS, GROUP * BANDS)
        return pltpu.make_async_copy(node_hbm.at[rows], node_ref.at[rows], node_sem.at[g])

    loads = [
        pltpu.make_async_copy(val_hbm, val_ref, in_sem.at[0]),
        pltpu.make_async_copy(grad_hbm, grad_ref, in_sem.at[1]),
    ]
    for load in loads:
        load.start()
    for g in range(groups):
        take(g).start()
    spread_ref[...] = jnp.broadcast_to(occ_ref[...], (BANDS, BANDS)).T
    table_ref[NODES - 7 :, :] = jnp.zeros((KPAD - NODES + 7, 4 * POINTS), BF16)
    loads[0].wait()
    table_ref[:NODES, :POINTS] = val_ref[...]
    loads[1].wait()
    for k in range(3):
        table_ref[:NODES, (k + 1) * POINTS : (k + 2) * POINTS] = grad_ref[k]
    leave = pltpu.make_async_copy(table_ref, table_hbm, out_sem)
    leave.start()

    for g in range(groups):
        slab = slab_ref.at[g % 2]
        rows = slice(g * GROUP * BANDS, (g + 1) * GROUP * BANDS)
        if g < 2:
            for later in range(g, groups if g else 1):
                take(later).wait()
        for k in range(4):
            slab[k] = jnp.dot(
                node_ref[rows, :], table_ref[:, k * POINTS : (k + 1) * POINTS], preferred_element_type=F32
            )
        for i in range(GROUP):
            c = g * GROUP + i
            bands = slice(i * BANDS, (i + 1) * BANDS)
            for q in range(RANKS):
                lead = slab[0, bands, lanes(q)]
                scaled = spread_ref[...] * lead
                sum_ref[q, 0, c : c + 1, :] = jnp.sum(scaled * lead, axis=0, keepdims=True)
                for k in range(1, 4):
                    term = slab[k, bands, lanes(q)]
                    sum_ref[q, k, c : c + 1, :] = 2.0 * jnp.sum(scaled * term, axis=0, keepdims=True)
    for d, part_ref in enumerate((part0_ref, part1_ref, part2_ref, part3_ref)):
        part_ref[...] = sum_ref[(band_ref[0] + d) & (RANKS - 1)]
    leave.wait()


def gradient_pass(band, occupancy, values, grads, cell_nodes):
    part = jax.ShapeDtypeStruct((4, CELLS, PART), F32)
    return pl.pallas_call(
        gradient_kernel,
        out_shape=(part, part, part, part, jax.ShapeDtypeStruct((KPAD, 4 * POINTS), BF16)),
        in_specs=[SM, VM] + [HB] * 3,
        out_specs=(VM, VM, VM, VM, HB),
        scratch_shapes=[
            pltpu.VMEM((NODES, POINTS), BF16),
            pltpu.VMEM((3, NODES, POINTS), BF16),
            pltpu.VMEM((CELLS * BANDS, KPAD), BF16),
            pltpu.VMEM((KPAD, 4 * POINTS), BF16),
            pltpu.VMEM((BANDS, BANDS), F32),
            pltpu.VMEM((2, 4, GROUP * BANDS, POINTS), F32),
            pltpu.VMEM((RANKS, 4, CELLS, PART), F32),
            pltpu.SemaphoreType.DMA((2,)),
            pltpu.SemaphoreType.DMA((CELLS // GROUP,)),
            pltpu.SemaphoreType.DMA,
        ],
        compiler_params=params(60),
        cost_estimate=cost(2 * 2048 * 512 * 3072, 8 * MIB),
        name="gradient_pass",
    )(band, occupancy, values, grads, cell_nodes)


def exchange_terms(density, square):
    third = jnp.exp(jnp.log(density) * (1.0 / 3.0))
    power_four = density * third
    reduced = reduced_coef * square / (power_four * power_four)
    inner = 1.0 + slope_coef * reduced / bound_kappa
    slope = slope_coef / (inner * inner)
    enhance = 1.0 + bound_kappa - bound_kappa / inner
    d_density = -slater_coef * third * ((4.0 / 3.0) * enhance - (8.0 / 3.0) * reduced * slope)
    d_square = -slater_coef * reduced_coef * slope / power_four
    return d_density, d_square


def exchange_kernel(wave_row_ref, slot_row_ref, came_ref, a_ref, b_ref, c_ref, d_ref, mix_ref, field_ref):
    for c in range(CELLS):
        row = wave_row_ref[c]
        for f in range(3):
            field_ref[f, c : c + 1, :] = came_ref[row, :, lanes(f)]
    total = [(a_ref[k] + b_ref[k]) + (c_ref[k] + d_ref[k]) for k in range(4)]
    core, weight, hartree = field_ref[0], field_ref[1], field_ref[2]
    square = total[1] * total[1] + total[2] * total[2] + total[3] * total[3]
    d_density, d_square = exchange_terms(core + total[0], square)
    mix_ref[:CELLS, :] = weight * (d_density + hartree)
    for k in range(1, 4):
        mix_ref[k * CELLS : (k + 1) * CELLS, :] = 2.0 * weight * d_square * total[k]
    for s in range(SLOTS):
        row = slot_row_ref[s]
        source = jnp.minimum(row, ROWS - 1)
        for q in range(RANKS):
            value = came_ref[source, :, FIELDS + q * PART : FIELDS + (q + 1) * PART]
            place = TERMS + q * SLOTS + s
            mix_ref[place : place + 1, :] = jnp.where(row < ROWS, value, 0.0)


def exchange(wave_rows, slot_rows, came, parts):
    return pl.pallas_call(
        exchange_kernel,
        out_shape=jax.ShapeDtypeStruct((MIX, PART), F32),
        in_specs=[SM, SM] + [VM] * 5,
        out_specs=VM,
        scratch_shapes=[pltpu.VMEM((3, CELLS, PART), F32)],
        compiler_params=params(8),
        cost_estimate=cost(1e6, MIB),
        name="exchange",
    )(wave_rows, slot_rows, came, *parts)


def second_kernel(
    band_ref, m0_ref, m1_ref, m2_ref, m3_ref, table_hbm, node_hbm, core_hbm, weight_hbm, shape_hbm, stiff_hbm,
    out_hbm, rest_hbm,
    wt_ref, node_ref, table_ref, slab_ref, prod_ref, wide_ref, out_ref,
    core_ref, weight_ref, shape_ref, stiff_ref, source_ref, in_sem, node_sem, out_sem, rest_sem,
):
    groups = CELLS // GROUP

    def take(g):
        rows = pl.ds(g * GROUP * BANDS, GROUP * BANDS)
        return pltpu.make_async_copy(node_hbm.at[rows], node_ref.at[rows], node_sem.at[g])

    load = pltpu.make_async_copy(table_hbm, table_ref, in_sem)
    load.start()
    for g in range(groups):
        take(g).start()
    rests = [
        pltpu.make_async_copy(core_hbm, core_ref, rest_sem.at[0]),
        pltpu.make_async_copy(weight_hbm, weight_ref, rest_sem.at[1]),
        pltpu.make_async_copy(shape_hbm, shape_ref, rest_sem.at[2]),
        pltpu.make_async_copy(stiff_hbm, stiff_ref, rest_sem.at[3]),
    ]
    for rest in rests:
        rest.start()
    for d, source in enumerate((m0_ref, m1_ref, m2_ref, m3_ref)):
        wt_ref[(band_ref[0] + RANKS - d) & (RANKS - 1)] = source[:TERMS, :]

    def evaluate(g, k):
        rows = slice(g * GROUP * BANDS, (g + 1) * GROUP * BANDS)
        slab_ref[g % 2, k] = jnp.dot(
            node_ref[rows, :], table_ref[:, k * POINTS : (k + 1) * POINTS], preferred_element_type=F32
        )

    def products(g, i):
        c = g * GROUP + i
        rows = slice(i * BANDS, (i + 1) * BANDS)
        for lane in range(RANKS):
            r = [wt_ref[lane, k * CELLS + c : k * CELLS + c + 1, :] for k in range(4)]
            q = [slab_ref[g % 2, k, rows, lanes(lane)] for k in range(4)]
            value = r[0] * q[0] + (r[1] * q[1] + r[2] * q[2] + r[3] * q[3])
            prod_ref[g % 2, rows, lanes(lane)] = value.astype(BF16)
            for k in range(1, 4):
                prod_ref[g % 2, rows, lanes(4 * k + lane)] = (r[k] * q[0]).astype(BF16)

    def multiply(g, pair):
        rows = slice(2 * pair * BANDS, 2 * (pair + 1) * BANDS)
        result = lax.dot_general(
            table_ref[:NODES, :], prod_ref[g % 2, rows, :], NT, preferred_element_type=F32
        )
        for i in range(2):
            c = g * GROUP + 2 * pair + i
            wide_ref[pl.ds(c, NODES, stride=CELLS), :] = result[:, i * BANDS : (i + 1) * BANDS]

    load.wait()
    take(0).wait()
    for k in range(4):
        evaluate(0, k)
    for g in range(1, groups):
        take(g).wait()
    for g in range(groups):
        for i in range(GROUP):
            if g + 1 < groups:
                evaluate(g + 1, i)
            products(g, i)
            if i % 2 == 1:
                multiply(g, i // 2)

    def leave(i):
        part = pl.ds(i * STEP, STEP)
        return pltpu.make_async_copy(out_ref.at[part], out_hbm.at[part], out_sem.at[i])

    for i in range(NODES // STEP):
        part = wide_ref[pl.ds(i * STEP * CELLS, STEP * CELLS), :].reshape(STEP, CELLS, BANDS)
        out_ref[pl.ds(i * STEP, STEP)] = part.astype(BF16)
        leave(i).start()

    for rest in rests:
        rest.wait()
    for q in range(RANKS):
        rows = slice(TERMS + q * SLOTS, TERMS + (q + 1) * SLOTS)
        dens = (m0_ref[rows, :] + m1_ref[rows, :]) + (m2_ref[rows, :] + m3_ref[rows, :])
        source_ref[:, lanes(q)] = weight_ref[:, lanes(q)] * (core_ref[:, lanes(q)] + dens)
    drawn = lax.dot_general(source_ref[...], shape_ref[...], NT, precision=HIGHEST, preferred_element_type=F32)
    stiff_ref[...] = stiff_ref[...] - drawn
    last = pltpu.make_async_copy(stiff_ref, rest_hbm, rest_sem.at[4])
    last.start()
    for i in range(NODES // STEP):
        leave(i).wait()
    last.wait()


def second_pass(band, mixes, table, cell_nodes, core, weight, shape, stiff):
    return pl.pallas_call(
        second_kernel,
        out_shape=(
            jax.ShapeDtypeStruct((NODES, CELLS, BANDS), BF16),
            jax.ShapeDtypeStruct((SLOTS, ENODES), F32),
        ),
        in_specs=[SM] + [VM] * 4 + [HB] * 6,
        out_specs=(HB, HB),
        scratch_shapes=[
            pltpu.VMEM((RANKS, TERMS, PART), F32),
            pltpu.VMEM((CELLS * BANDS, KPAD), BF16),
            pltpu.VMEM((KPAD, 4 * POINTS), BF16),
            pltpu.VMEM((2, 4, GROUP * BANDS, POINTS), F32),
            pltpu.VMEM((2, GROUP * BANDS, 4 * POINTS), BF16),
            pltpu.VMEM((NODES * CELLS, BANDS), F32),
            pltpu.VMEM((NODES, CELLS, BANDS), BF16),
            pltpu.VMEM((SLOTS, POINTS), F32),
            pltpu.VMEM((SLOTS, POINTS), F32),
            pltpu.VMEM((ENODES, POINTS), F32),
            pltpu.VMEM((SLOTS, ENODES), F32),
            pltpu.VMEM((SLOTS, POINTS), F32),
            pltpu.SemaphoreType.DMA,
            pltpu.SemaphoreType.DMA((CELLS // GROUP,)),
            pltpu.SemaphoreType.DMA((NODES // STEP,)),
            pltpu.SemaphoreType.DMA((5,)),
        ],
        compiler_params=params(60),
        cost_estimate=cost(4 * 2048 * 512 * 3072, 8 * MIB),
        name="second_pass",
    )(band, *mixes, table, cell_nodes, core, weight, shape, stiff)


def stiff_kernel(nodes_ref, stiff_ref, scale_ref, out_ref):
    product = lax.dot_general(nodes_ref[...], stiff_ref[...], NT, precision=HIGHEST, preferred_element_type=F32)
    spread = jnp.broadcast_to(scale_ref[...], (128, SLOTS)).T
    for j in range(0, ENODES, 128):
        width = min(128, ENODES - j)
        out_ref[:, j : j + width] = product[:, j : j + width] * spread[:, :width]


def stiff_part(nodes, stiffness, scale):
    return pl.pallas_call(
        stiff_kernel,
        out_shape=jax.ShapeDtypeStruct((SLOTS, ENODES), F32),
        in_specs=[VM] * 3,
        out_specs=VM,
        compiler_params=params(12),
        cost_estimate=cost(12 * SLOTS * ENODES * ENODES, 3 * MIB),
        name="stiff_part",
    )(nodes, stiffness, scale)


def shift(array, distance):
    return lax.ppermute(array, "band", [(i, (i + distance) % RANKS) for i in range(RANKS)])


def body(
    orbitals, occupancy, shape_values, shape_grads, cell_slot, slot_cell, potential_nodes,
    stiffness, stiff_scale, electro_shape, core_density, quad_weight,
):
    values, grads = shape_values.T, shape_grads.transpose(0, 2, 1)
    nodes, shape = potential_nodes.T, electro_shape.T
    occupancy = occupancy.reshape(1, BANDS)
    band = lax.axis_index("band").astype(I32).reshape(1)

    send, cell_nodes, wave_rows, slot_rows = first_pass(
        band, slot_cell, cell_slot, orbitals, occupancy, values, nodes, shape, core_density, quad_weight
    )
    came = lax.all_to_all(send, "dom", split_axis=0, concat_axis=0, tiled=True)
    *parts, table = gradient_pass(band, occupancy, values, grads, cell_nodes)
    parts = [parts[0]] + [shift(parts[d], d) for d in (1, 2, 3)]
    stiff = stiff_part(nodes, stiffness, stiff_scale.reshape(1, SLOTS))
    mix = exchange(wave_rows, slot_rows, came, parts)
    mixes = [mix] + [shift(mix, d) for d in (1, 2, 3)]
    action, rest = second_pass(band, mixes, table, cell_nodes, core_density, quad_weight, shape, stiff)
    return action, rest.T


def solution(mesh):
    return jax.shard_map(
        body,
        mesh=mesh,
        in_specs=(
            P(None, "dom", "band"), P("band"), P(), P(), P("dom"), P("dom"),
            P(None, "dom"), P(), P("dom"), P(), P("dom", None), P("dom", None),
        ),
        out_specs=(P(None, "dom", "band"), P(None, "dom")),
        check_vma=False,
    )
```

```python
import functools

import jax
import jax.numpy as jnp
from jax import lax
from jax.experimental import pallas as pl
from jax.experimental.pallas import tpu as pltpu
from jax.sharding import PartitionSpec as P

F32, BF16, I32 = jnp.float32, jnp.bfloat16, jnp.int32
NODES, CELLS, BANDS, POINTS = 343, 24, 128, 512
KPAD = 384
SLOTS, ENODES, DOMAINS, CAP = 48, 729, 64, 2
ROWS = DOMAINS * CAP
RANKS, PART = 4, 128
GROUP = 4
STEP = 49
FIELDS = 3 * PART
WIDTH = FIELDS + POINTS
TERMS = 4 * CELLS
MIX = TERMS + RANKS * SLOTS
EXACT = lax.Precision.HIGH
NT = (((1,), (1,)), ((), ()))
MIB = 1 << 20

slater_coef = 0.7385587663820224
bound_kappa = 0.804
slope_coef = 0.2195149727645171
reduced_coef = 0.026121172985233605

VM = pl.BlockSpec(memory_space=pltpu.VMEM)
SM = pl.BlockSpec(memory_space=pltpu.SMEM)
HB = pl.BlockSpec(memory_space=pltpu.HBM)


def params(mib):
    return pltpu.CompilerParams(vmem_limit_bytes=mib * MIB)


def cost(flops, nbytes):
    return pl.CostEstimate(flops=int(flops), bytes_accessed=int(nbytes), transcendentals=0)


def lanes(index):
    return slice(index * 128, index * 128 + 128)


def first_kernel(
    band_ref, slot_cell_ref, cell_slot_ref,
    orb_hbm, occ_ref, val_hbm, nodes_hbm, shape_hbm, core_hbm, weight_hbm,
    send_hbm, node_hbm, wave_row_ref, slot_row_ref,
    orb_ref, val_ref, nodes_ref, shape_ref, field_ref, send_ref,
    wide_ref, node_ref, table_ref, spread_ref, sum_ref, count_ref, in_sem, orb_sem, out_sem, send_sem,
):
    mine = pl.ds(pl.multiple_of(band_ref[0] * PART, PART), PART)
    chunks = NODES // STEP

    def take(i):
        part = pl.ds(i * STEP, STEP)
        return pltpu.make_async_copy(orb_hbm.at[part], orb_ref.at[part], orb_sem.at[i])

    loads = [
        pltpu.make_async_copy(val_hbm, val_ref, in_sem.at[0]),
        pltpu.make_async_copy(nodes_hbm, nodes_ref, in_sem.at[1]),
        pltpu.make_async_copy(shape_hbm.at[:, mine], shape_ref, in_sem.at[2]),
        pltpu.make_async_copy(core_hbm.at[:, mine], field_ref.at[:, lanes(0)], in_sem.at[3]),
        pltpu.make_async_copy(weight_hbm.at[:, mine], field_ref.at[:, lanes(1)], in_sem.at[4]),
    ]
    for load in loads:
        load.start()
    for i in range(chunks):
        take(i).start()

    for d in range(DOMAINS + 1):
        count_ref[d] = 0
    for s in range(SLOTS):
        cell = slot_cell_ref[s]
        filled = cell >= 0
        source = jnp.where(filled, lax.shift_right_logical(cell * 10923, 18), DOMAINS)
        place = jnp.minimum(count_ref[source], CAP - 1)
        count_ref[source] = jnp.where(filled, place + 1, 0)
        slot_row_ref[s] = jnp.where(filled, source * CAP + place, ROWS)
    for d in range(DOMAINS):
        count_ref[d] = -1
    for c in range(CELLS):
        slot = cell_slot_ref[c]
        owner = lax.shift_right_logical(slot * 21846, 20)
        other = count_ref[owner]
        known = other >= 0
        first = jnp.maximum(other, 0)
        later = known & (cell_slot_ref[first] > slot)
        wave_row_ref[c] = owner * CAP + jnp.where(known & jnp.logical_not(later), 1, 0)
        target = jnp.where(later, first, c)
        wave_row_ref[target] = jnp.where(later, owner * CAP + 1, wave_row_ref[c])
        count_ref[owner] = c

    spread_ref[...] = jnp.broadcast_to(occ_ref[...], (BANDS, BANDS)).T
    table_ref[NODES - 7 :, :] = jnp.zeros((KPAD - NODES + 7, POINTS), BF16)
    wide_ref[NODES * CELLS :, :] = jnp.zeros(((KPAD - NODES) * CELLS, BANDS), F32)

    for load in loads:
        load.wait()
    table_ref[:NODES, :] = val_ref[...]
    field_ref[:, lanes(2)] = jnp.dot(
        nodes_ref[...], shape_ref[...], precision=EXACT, preferred_element_type=F32
    )
    for s in range(SLOTS):
        send_ref[slot_row_ref[s], :, :FIELDS] = field_ref[s : s + 1, :]

    for i in range(chunks):
        take(i).wait()
        part = orb_ref[pl.ds(i * STEP, STEP)].astype(F32)
        wide_ref[pl.ds(i * STEP * CELLS, STEP * CELLS), :] = part.reshape(STEP * CELLS, BANDS)

    def store(g):
        rows = pl.ds(g * GROUP * BANDS, GROUP * BANDS)
        return pltpu.make_async_copy(node_ref.at[rows], node_hbm.at[rows], out_sem.at[g])

    groups = CELLS // GROUP
    for g in range(groups):
        rows = slice(g * GROUP * BANDS, (g + 1) * GROUP * BANDS)
        for i in range(GROUP):
            c = g * GROUP + i
            block = wide_ref[pl.ds(c, KPAD, stride=CELLS), :]
            node_ref[c * BANDS : (c + 1) * BANDS, :] = block.T.astype(BF16)
        store(g).start()
        values = jnp.dot(node_ref[rows, :], table_ref[...], preferred_element_type=F32)
        for i in range(GROUP):
            c = g * GROUP + i
            for q in range(RANKS):
                lead = values[i * BANDS : (i + 1) * BANDS, lanes(q)]
                sum_ref[c : c + 1, lanes(q)] = jnp.sum(spread_ref[...] * lead * lead, axis=0, keepdims=True)
    for c in range(CELLS):
        send_ref[wave_row_ref[c], :, FIELDS:] = sum_ref[c : c + 1, :]
    leave = pltpu.make_async_copy(send_ref.at[pl.ds(0, ROWS)], send_hbm, send_sem)
    leave.start()
    for g in range(groups):
        store(g).wait()
    leave.wait()


def first_pass(band, slot_cell, cell_slot, orbitals, occupancy, values, nodes, shape, core, weight):
    return pl.pallas_call(
        first_kernel,
        out_shape=(
            jax.ShapeDtypeStruct((ROWS, 1, WIDTH), F32),
            jax.ShapeDtypeStruct((CELLS * BANDS, KPAD), BF16),
            jax.ShapeDtypeStruct((CELLS,), I32),
            jax.ShapeDtypeStruct((SLOTS,), I32),
        ),
        in_specs=[SM, SM, SM, HB, VM] + [HB] * 5,
        out_specs=(HB, HB, SM, SM),
        scratch_shapes=[
            pltpu.VMEM((NODES, CELLS, BANDS), BF16),
            pltpu.VMEM((NODES, POINTS), BF16),
            pltpu.VMEM((SLOTS, ENODES), F32),
            pltpu.VMEM((ENODES, PART), F32),
            pltpu.VMEM((SLOTS, FIELDS), F32),
            pltpu.VMEM((ROWS + 1, 1, WIDTH), F32),
            pltpu.VMEM((KPAD * CELLS, BANDS), F32),
            pltpu.VMEM((CELLS * BANDS, KPAD), BF16),
            pltpu.VMEM((KPAD, POINTS), BF16),
            pltpu.VMEM((BANDS, BANDS), F32),
            pltpu.VMEM((CELLS, POINTS), F32),
            pltpu.SMEM((DOMAINS + 1,), I32),
            pltpu.SemaphoreType.DMA((5,)),
            pltpu.SemaphoreType.DMA((NODES // STEP,)),
            pltpu.SemaphoreType.DMA((CELLS // GROUP,)),
            pltpu.SemaphoreType.DMA,
        ],
        compiler_params=params(60),
        cost_estimate=cost(2 * 512 * 512 * 3072, 8 * MIB),
        name="first_pass",
    )(band, slot_cell, cell_slot, orbitals, occupancy, values, nodes, shape, core, weight)


def gradient_kernel(
    band_ref, occ_ref, val_hbm, grad_hbm, node_hbm,
    part0_ref, part1_ref, part2_ref, part3_ref,
    table_ref, node_ref, spread_ref, slab_ref, sum_ref, table_sem, node_sem,
):
    groups = CELLS // GROUP

    def take(g):
        rows = pl.ds(g * GROUP * BANDS, GROUP * BANDS)
        return pltpu.make_async_copy(node_hbm.at[rows], node_ref.at[rows], node_sem.at[g])

    tables = [pltpu.make_async_copy(val_hbm, table_ref.at[0], table_sem.at[0])]
    for k in range(3):
        tables.append(pltpu.make_async_copy(grad_hbm.at[k], table_ref.at[k + 1], table_sem.at[k + 1]))
    tables[0].start()
    take(0).start()
    for k in range(1, 4):
        tables[k].start()
    for g in range(1, groups):
        take(g).start()
    spread_ref[...] = jnp.broadcast_to(occ_ref[...], (BANDS, BANDS)).T
    take(0).wait()

    for g in range(groups):
        slab = slab_ref.at[g % 2]
        rows = slice(g * GROUP * BANDS, (g + 1) * GROUP * BANDS)
        if g == 1:
            for later in range(1, groups):
                take(later).wait()
        for k in range(4):
            if g == 0:
                tables[k].wait()
            slab[k] = jnp.dot(node_ref[rows, :NODES], table_ref[k], preferred_element_type=F32)
        for i in range(GROUP):
            c = g * GROUP + i
            bands = slice(i * BANDS, (i + 1) * BANDS)
            for q in range(RANKS):
                lead = slab[0, bands, lanes(q)]
                scaled = spread_ref[...] * lead
                sum_ref[q, 0, c : c + 1, :] = jnp.sum(scaled * lead, axis=0, keepdims=True)
                for k in range(1, 4):
                    term = slab[k, bands, lanes(q)]
                    sum_ref[q, k, c : c + 1, :] = 2.0 * jnp.sum(scaled * term, axis=0, keepdims=True)
    for d, part_ref in enumerate((part0_ref, part1_ref, part2_ref, part3_ref)):
        part_ref[...] = sum_ref[(band_ref[0] + d) & (RANKS - 1)]


def gradient_pass(band, occupancy, values, grads, cell_nodes):
    part = jax.ShapeDtypeStruct((4, CELLS, PART), F32)
    return pl.pallas_call(
        gradient_kernel,
        out_shape=(part, part, part, part),
        in_specs=[SM, VM] + [HB] * 3,
        out_specs=(VM, VM, VM, VM),
        scratch_shapes=[
            pltpu.VMEM((4, NODES, POINTS), BF16),
            pltpu.VMEM((CELLS * BANDS, KPAD), BF16),
            pltpu.VMEM((BANDS, BANDS), F32),
            pltpu.VMEM((2, 4, GROUP * BANDS, POINTS), F32),
            pltpu.VMEM((RANKS, 4, CELLS, PART), F32),
            pltpu.SemaphoreType.DMA((4,)),
            pltpu.SemaphoreType.DMA((CELLS // GROUP,)),
        ],
        compiler_params=params(60),
        cost_estimate=cost(2 * 2048 * 512 * 3072, 8 * MIB),
        name="gradient_pass",
    )(band, occupancy, values, grads, cell_nodes)


def exchange_terms(density, square):
    third = jnp.exp(jnp.log(density) * (1.0 / 3.0))
    power_four = density * third
    reduced = reduced_coef * square / (power_four * power_four)
    inner = 1.0 + slope_coef * reduced / bound_kappa
    slope = slope_coef / (inner * inner)
    enhance = 1.0 + bound_kappa - bound_kappa / inner
    d_density = -slater_coef * third * ((4.0 / 3.0) * enhance - (8.0 / 3.0) * reduced * slope)
    d_square = -slater_coef * reduced_coef * slope / power_four
    return d_density, d_square


def gather_kernel(wave_row_ref, slot_row_ref, came_ref, field_ref, dens_ref):
    for c in range(CELLS):
        row = wave_row_ref[c]
        for f in range(3):
            place = f * CELLS + c
            field_ref[place : place + 1, :] = came_ref[row, :, lanes(f)]
    for s in range(SLOTS):
        row = slot_row_ref[s]
        source = jnp.minimum(row, ROWS - 1)
        for q in range(RANKS):
            value = came_ref[source, :, FIELDS + q * PART : FIELDS + (q + 1) * PART]
            place = q * SLOTS + s
            dens_ref[place : place + 1, :] = jnp.where(row < ROWS, value, 0.0)


def gather(wave_rows, slot_rows, came):
    return pl.pallas_call(
        gather_kernel,
        out_shape=(
            jax.ShapeDtypeStruct((3 * CELLS, PART), F32),
            jax.ShapeDtypeStruct((RANKS * SLOTS, PART), F32),
        ),
        in_specs=[SM, SM, VM],
        out_specs=(VM, VM),
        compiler_params=params(8),
        cost_estimate=cost(1e6, MIB),
        name="gather",
    )(wave_rows, slot_rows, came)


def exchange_kernel(field_ref, dens_ref, a_ref, b_ref, c_ref, d_ref, mix_ref):
    total = [(a_ref[k] + b_ref[k]) + (c_ref[k] + d_ref[k]) for k in range(4)]
    core, weight, hartree = [field_ref[f * CELLS : (f + 1) * CELLS, :] for f in range(3)]
    square = total[1] * total[1] + total[2] * total[2] + total[3] * total[3]
    d_density, d_square = exchange_terms(core + total[0], square)
    mix_ref[:CELLS, :] = weight * (d_density + hartree)
    for k in range(1, 4):
        mix_ref[k * CELLS : (k + 1) * CELLS, :] = 2.0 * weight * d_square * total[k]
    mix_ref[TERMS:, :] = dens_ref[...]


def exchange(field, dens, parts):
    return pl.pallas_call(
        exchange_kernel,
        out_shape=jax.ShapeDtypeStruct((MIX, PART), F32),
        in_specs=[VM] * 6,
        out_specs=VM,
        compiler_params=params(8),
        cost_estimate=cost(1e6, MIB),
        name="exchange",
    )(field, dens, *parts)


def second_kernel(
    band_ref, m0_ref, m1_ref, m2_ref, m3_ref, val_ref, grad_ref, node_ref,
    core_ref, weight_ref, shape_ref, stiff_ref, val_hbm, grad_hbm,
    out_hbm, rest_ref,
    wt_ref, table_ref, slab_ref, prod_ref, wide_ref, out_ref, source_ref, table_sem, out_sem,
):
    groups = CELLS // GROUP
    tables = [pltpu.make_async_copy(val_hbm, table_ref.at[:, :POINTS], table_sem.at[0])]
    for k in range(3):
        tables.append(
            pltpu.make_async_copy(
                grad_hbm.at[k], table_ref.at[:, (k + 1) * POINTS : (k + 2) * POINTS], table_sem.at[k + 1]
            )
        )
    for table in tables:
        table.start()
    for d, source in enumerate((m0_ref, m1_ref, m2_ref, m3_ref)):
        wt_ref[(band_ref[0] + RANKS - d) & (RANKS - 1)] = source[:TERMS, :]

    def evaluate(g, k):
        rows = slice(g * GROUP * BANDS, (g + 1) * GROUP * BANDS)
        slab_ref[g % 2, k] = jnp.dot(
            node_ref[rows, :NODES], grad_ref[k - 1] if k else val_ref[...], preferred_element_type=F32
        )

    def products(g, i):
        c = g * GROUP + i
        rows = slice(i * BANDS, (i + 1) * BANDS)
        for lane in range(RANKS):
            r = [wt_ref[lane, k * CELLS + c : k * CELLS + c + 1, :] for k in range(4)]
            q = [slab_ref[g % 2, k, rows, lanes(lane)] for k in range(4)]
            value = r[0] * q[0] + (r[1] * q[1] + r[2] * q[2] + r[3] * q[3])
            prod_ref[g % 2, rows, lanes(lane)] = value.astype(BF16)
            for k in range(1, 4):
                prod_ref[g % 2, rows, lanes(4 * k + lane)] = (r[k] * q[0]).astype(BF16)

    def multiply(g, pair):
        rows = slice(2 * pair * BANDS, 2 * (pair + 1) * BANDS)
        result = lax.dot_general(
            table_ref[...], prod_ref[g % 2, rows, :], NT, preferred_element_type=F32
        )
        for i in range(2):
            c = g * GROUP + 2 * pair + i
            wide_ref[pl.ds(c, NODES, stride=CELLS), :] = result[:, i * BANDS : (i + 1) * BANDS]

    for k in range(4):
        evaluate(0, k)
    for table in tables:
        table.wait()
    for g in range(groups):
        for i in range(GROUP):
            if g + 1 < groups:
                evaluate(g + 1, i)
            products(g, i)
            if i % 2 == 1:
                multiply(g, i // 2)

    def leave(i):
        part = pl.ds(i * STEP, STEP)
        return pltpu.make_async_copy(out_ref.at[part], out_hbm.at[part], out_sem.at[i])

    for i in range(NODES // STEP):
        part = wide_ref[pl.ds(i * STEP * CELLS, STEP * CELLS), :].reshape(STEP, CELLS, BANDS)
        out_ref[pl.ds(i * STEP, STEP)] = part.astype(BF16)
        leave(i).start()

    for q in range(RANKS):
        rows = slice(TERMS + q * SLOTS, TERMS + (q + 1) * SLOTS)
        dens = (m0_ref[rows, :] + m1_ref[rows, :]) + (m2_ref[rows, :] + m3_ref[rows, :])
        source_ref[:, lanes(q)] = weight_ref[:, lanes(q)] * (core_ref[:, lanes(q)] + dens)
    drawn = lax.dot_general(source_ref[...], shape_ref[...], NT, precision=EXACT, preferred_element_type=F32)
    rest_ref[...] = stiff_ref[...] - drawn
    for i in range(NODES // STEP):
        leave(i).wait()


def second_pass(band, mixes, values, grads, cell_nodes, core, weight, shape, stiff):
    return pl.pallas_call(
        second_kernel,
        out_shape=(
            jax.ShapeDtypeStruct((NODES, CELLS, BANDS), BF16),
            jax.ShapeDtypeStruct((SLOTS, ENODES), F32),
        ),
        in_specs=[SM] + [VM] * 11 + [HB] * 2,
        out_specs=(HB, VM),
        scratch_shapes=[
            pltpu.VMEM((RANKS, TERMS, PART), F32),
            pltpu.VMEM((NODES, 4 * POINTS), BF16),
            pltpu.VMEM((2, 4, GROUP * BANDS, POINTS), F32),
            pltpu.VMEM((2, GROUP * BANDS, 4 * POINTS), BF16),
            pltpu.VMEM((NODES * CELLS, BANDS), F32),
            pltpu.VMEM((NODES, CELLS, BANDS), BF16),
            pltpu.VMEM((SLOTS, POINTS), F32),
            pltpu.SemaphoreType.DMA((4,)),
            pltpu.SemaphoreType.DMA((NODES // STEP,)),
        ],
        compiler_params=params(36),
        cost_estimate=cost(4 * 2048 * 512 * 3072, 8 * MIB),
        name="second_pass",
    )(band, *mixes, values, grads, cell_nodes, core, weight, shape, stiff, values, grads)


def stiff_kernel(nodes_ref, stiff_ref, scale_ref, out_ref):
    product = lax.dot_general(nodes_ref[...], stiff_ref[...], NT, precision=EXACT, preferred_element_type=F32)
    spread = jnp.broadcast_to(scale_ref[...], (128, SLOTS)).T
    for j in range(0, ENODES, 128):
        width = min(128, ENODES - j)
        out_ref[:, j : j + width] = product[:, j : j + width] * spread[:, :width]


def stiff_part(nodes, stiffness, scale):
    return pl.pallas_call(
        stiff_kernel,
        out_shape=jax.ShapeDtypeStruct((SLOTS, ENODES), F32),
        in_specs=[VM] * 3,
        out_specs=VM,
        compiler_params=params(12),
        cost_estimate=cost(12 * SLOTS * ENODES * ENODES, 3 * MIB),
        name="stiff_part",
    )(nodes, stiffness, scale)


def shift(array, distance):
    return lax.ppermute(array, "band", [(i, (i + distance) % RANKS) for i in range(RANKS)])


def body(
    orbitals, occupancy, shape_values, shape_grads, cell_slot, slot_cell, potential_nodes,
    stiffness, stiff_scale, electro_shape, core_density, quad_weight,
):
    values, grads = shape_values.T, shape_grads.transpose(0, 2, 1)
    nodes, shape = potential_nodes.T, electro_shape.T
    occupancy = occupancy.reshape(1, BANDS)
    band = lax.axis_index("band").astype(I32).reshape(1)

    send, cell_nodes, wave_rows, slot_rows = first_pass(
        band, slot_cell, cell_slot, orbitals, occupancy, values, nodes, shape, core_density, quad_weight
    )
    came = lax.all_to_all(send, "dom", split_axis=0, concat_axis=0, tiled=True)
    parts = gradient_pass(band, occupancy, values, grads, cell_nodes)
    parts = [parts[0]] + [shift(parts[d], d) for d in (1, 2, 3)]
    stiff = stiff_part(nodes, stiffness, stiff_scale.reshape(1, SLOTS))
    field, dens = gather(wave_rows, slot_rows, came)
    mix = exchange(field, dens, parts)
    mixes = [mix] + [shift(mix, d) for d in (1, 2, 3)]
    action, rest = second_pass(
        band, mixes, values, grads, cell_nodes, core_density, quad_weight, shape, stiff
    )
    return action, rest.T


def solution(mesh):
    return jax.shard_map(
        body,
        mesh=mesh,
        in_specs=(
            P(None, "dom", "band"), P("band"), P(), P(), P("dom"), P("dom"),
            P(None, "dom"), P(), P("dom"), P(), P("dom", None), P("dom", None),
        ),
        out_specs=(P(None, "dom", "band"), P(None, "dom")),
        check_vma=False,
    )
```

```python
import functools

import jax
import jax.numpy as jnp
from jax import lax
from jax.experimental import pallas as pl
from jax.experimental.pallas import tpu as pltpu
from jax.sharding import PartitionSpec as P

F32, BF16, I32 = jnp.float32, jnp.bfloat16, jnp.int32
NODES, CELLS, BANDS, POINTS = 343, 24, 128, 512
KPAD = 384
SLOTS, ENODES, DOMAINS, CAP = 48, 729, 64, 2
ROWS = DOMAINS * CAP
RANKS, PART = 4, 128
GROUP = 4
STEP = 49
FIELDS = 3 * PART
WIDTH = FIELDS + POINTS
HELD = 3 * CELLS
MIX = HELD + RANKS * SLOTS
EXACT = lax.Precision.HIGH
NT = (((1,), (1,)), ((), ()))
MIB = 1 << 20

slater_coef = 0.7385587663820224
bound_kappa = 0.804
slope_coef = 0.2195149727645171
reduced_coef = 0.026121172985233605

VM = pl.BlockSpec(memory_space=pltpu.VMEM)
SM = pl.BlockSpec(memory_space=pltpu.SMEM)
HB = pl.BlockSpec(memory_space=pltpu.HBM)


def params(mib):
    return pltpu.CompilerParams(vmem_limit_bytes=mib * MIB)


def cost(flops, nbytes):
    return pl.CostEstimate(flops=int(flops), bytes_accessed=int(nbytes), transcendentals=0)


def lanes(index):
    return slice(index * 128, index * 128 + 128)


def first_kernel(
    band_ref, slot_cell_ref, cell_slot_ref,
    orb_hbm, occ_ref, val_hbm, nodes_hbm, shape_hbm, core_hbm, weight_hbm,
    send_hbm, node_hbm, wave_row_ref, slot_row_ref,
    orb_ref, val_ref, nodes_ref, shape_ref, field_ref, send_ref,
    wide_ref, node_ref, table_ref, spread_ref, sum_ref, count_ref, in_sem, orb_sem, out_sem, send_sem,
):
    mine = pl.ds(pl.multiple_of(band_ref[0] * PART, PART), PART)
    chunks = NODES // STEP

    def take(i):
        part = pl.ds(i * STEP, STEP)
        return pltpu.make_async_copy(orb_hbm.at[part], orb_ref.at[part], orb_sem.at[i])

    loads = [
        pltpu.make_async_copy(val_hbm, val_ref, in_sem.at[0]),
        pltpu.make_async_copy(nodes_hbm, nodes_ref, in_sem.at[1]),
        pltpu.make_async_copy(shape_hbm.at[:, mine], shape_ref, in_sem.at[2]),
        pltpu.make_async_copy(core_hbm.at[:, mine], field_ref.at[:, lanes(0)], in_sem.at[3]),
        pltpu.make_async_copy(weight_hbm.at[:, mine], field_ref.at[:, lanes(1)], in_sem.at[4]),
    ]
    for load in loads:
        load.start()
    for i in range(chunks):
        take(i).start()

    for d in range(DOMAINS + 1):
        count_ref[d] = 0
    for s in range(SLOTS):
        cell = slot_cell_ref[s]
        filled = cell >= 0
        source = jnp.where(filled, lax.shift_right_logical(cell * 10923, 18), DOMAINS)
        place = jnp.minimum(count_ref[source], CAP - 1)
        count_ref[source] = jnp.where(filled, place + 1, 0)
        slot_row_ref[s] = jnp.where(filled, source * CAP + place, ROWS)
    for d in range(DOMAINS):
        count_ref[d] = -1
    for c in range(CELLS):
        slot = cell_slot_ref[c]
        owner = lax.shift_right_logical(slot * 21846, 20)
        other = count_ref[owner]
        known = other >= 0
        first = jnp.maximum(other, 0)
        later = known & (cell_slot_ref[first] > slot)
        wave_row_ref[c] = owner * CAP + jnp.where(known & jnp.logical_not(later), 1, 0)
        target = jnp.where(later, first, c)
        wave_row_ref[target] = jnp.where(later, owner * CAP + 1, wave_row_ref[c])
        count_ref[owner] = c

    spread_ref[...] = jnp.broadcast_to(occ_ref[...], (BANDS, BANDS)).T
    table_ref[NODES - 7 :, :] = jnp.zeros((KPAD - NODES + 7, POINTS), BF16)
    wide_ref[NODES * CELLS :, :] = jnp.zeros(((KPAD - NODES) * CELLS, BANDS), F32)

    for load in loads:
        load.wait()
    table_ref[:NODES, :] = val_ref[...]
    field_ref[:, lanes(2)] = jnp.dot(
        nodes_ref[...], shape_ref[...], precision=EXACT, preferred_element_type=F32
    )
    for s in range(SLOTS):
        send_ref[slot_row_ref[s], :, :FIELDS] = field_ref[s : s + 1, :]

    for i in range(chunks):
        take(i).wait()
        part = orb_ref[pl.ds(i * STEP, STEP)].astype(F32)
        wide_ref[pl.ds(i * STEP * CELLS, STEP * CELLS), :] = part.reshape(STEP * CELLS, BANDS)

    def store(g):
        rows = pl.ds(g * GROUP * BANDS, GROUP * BANDS)
        return pltpu.make_async_copy(node_ref.at[rows], node_hbm.at[rows], out_sem.at[g])

    groups = CELLS // GROUP
    for g in range(groups):
        rows = slice(g * GROUP * BANDS, (g + 1) * GROUP * BANDS)
        for i in range(GROUP):
            c = g * GROUP + i
            block = wide_ref[pl.ds(c, KPAD, stride=CELLS), :]
            node_ref[c * BANDS : (c + 1) * BANDS, :] = block.T.astype(BF16)
        store(g).start()
        values = jnp.dot(node_ref[rows, :], table_ref[...], preferred_element_type=F32)
        for i in range(GROUP):
            c = g * GROUP + i
            for q in range(RANKS):
                lead = values[i * BANDS : (i + 1) * BANDS, lanes(q)]
                sum_ref[c : c + 1, lanes(q)] = jnp.sum(spread_ref[...] * lead * lead, axis=0, keepdims=True)
    for c in range(CELLS):
        send_ref[wave_row_ref[c], :, FIELDS:] = sum_ref[c : c + 1, :]
    leave = pltpu.make_async_copy(send_ref.at[pl.ds(0, ROWS)], send_hbm, send_sem)
    leave.start()
    for g in range(groups):
        store(g).wait()
    leave.wait()


def first_pass(band, slot_cell, cell_slot, orbitals, occupancy, values, nodes, shape, core, weight):
    return pl.pallas_call(
        first_kernel,
        out_shape=(
            jax.ShapeDtypeStruct((ROWS, 1, WIDTH), F32),
            jax.ShapeDtypeStruct((CELLS * BANDS, KPAD), BF16),
            jax.ShapeDtypeStruct((CELLS,), I32),
            jax.ShapeDtypeStruct((SLOTS,), I32),
        ),
        in_specs=[SM, SM, SM, HB, VM] + [HB] * 5,
        out_specs=(HB, HB, SM, SM),
        scratch_shapes=[
            pltpu.VMEM((NODES, CELLS, BANDS), BF16),
            pltpu.VMEM((NODES, POINTS), BF16),
            pltpu.VMEM((SLOTS, ENODES), F32),
            pltpu.VMEM((ENODES, PART), F32),
            pltpu.VMEM((SLOTS, FIELDS), F32),
            pltpu.VMEM((ROWS + 1, 1, WIDTH), F32),
            pltpu.VMEM((KPAD * CELLS, BANDS), F32),
            pltpu.VMEM((CELLS * BANDS, KPAD), BF16),
            pltpu.VMEM((KPAD, POINTS), BF16),
            pltpu.VMEM((BANDS, BANDS), F32),
            pltpu.VMEM((CELLS, POINTS), F32),
            pltpu.SMEM((DOMAINS + 1,), I32),
            pltpu.SemaphoreType.DMA((5,)),
            pltpu.SemaphoreType.DMA((NODES // STEP,)),
            pltpu.SemaphoreType.DMA((CELLS // GROUP,)),
            pltpu.SemaphoreType.DMA,
        ],
        compiler_params=params(60),
        cost_estimate=cost(2 * 512 * 512 * 3072, 8 * MIB),
        name="first_pass",
    )(band, slot_cell, cell_slot, orbitals, occupancy, values, nodes, shape, core, weight)


def gradient_kernel(
    occ_ref, val_hbm, grad_hbm, node_hbm, part_ref,
    table_ref, node_ref, spread_ref, slab_ref, table_sem, node_sem,
):
    groups = CELLS // GROUP

    def take(g):
        rows = pl.ds(g * GROUP * BANDS, GROUP * BANDS)
        return pltpu.make_async_copy(node_hbm.at[rows], node_ref.at[rows], node_sem.at[g])

    tables = [pltpu.make_async_copy(val_hbm, table_ref.at[0], table_sem.at[0])]
    for k in range(3):
        tables.append(pltpu.make_async_copy(grad_hbm.at[k], table_ref.at[k + 1], table_sem.at[k + 1]))
    tables[0].start()
    take(0).start()
    for k in range(1, 4):
        tables[k].start()
    for g in range(1, groups):
        take(g).start()
    spread_ref[...] = jnp.broadcast_to(occ_ref[...], (BANDS, BANDS)).T
    take(0).wait()

    def evaluate(g, k):
        rows = slice(g * GROUP * BANDS, (g + 1) * GROUP * BANDS)
        slab_ref[g % 2, k] = jnp.dot(node_ref[rows, :NODES], table_ref[k], preferred_element_type=F32)

    def reduce(g, i):
        c = g * GROUP + i
        bands = slice(i * BANDS, (i + 1) * BANDS)
        for q in range(RANKS):
            lead = slab_ref[g % 2, 0, bands, lanes(q)]
            scaled = spread_ref[...] * lead
            part_ref[0, c : c + 1, lanes(q)] = jnp.sum(scaled * lead, axis=0, keepdims=True)
            for k in range(1, 4):
                term = slab_ref[g % 2, k, bands, lanes(q)]
                part_ref[k, c : c + 1, lanes(q)] = 2.0 * jnp.sum(scaled * term, axis=0, keepdims=True)

    for k in range(4):
        tables[k].wait()
        evaluate(0, k)
    for g in range(1, groups):
        take(g).wait()
    for g in range(groups):
        for i in range(GROUP):
            if g + 1 < groups:
                evaluate(g + 1, i)
            reduce(g, i)


def gradient_pass(occupancy, values, grads, cell_nodes):
    return pl.pallas_call(
        gradient_kernel,
        out_shape=jax.ShapeDtypeStruct((4, CELLS, POINTS), F32),
        in_specs=[VM] + [HB] * 3,
        out_specs=VM,
        scratch_shapes=[
            pltpu.VMEM((4, NODES, POINTS), BF16),
            pltpu.VMEM((CELLS * BANDS, KPAD), BF16),
            pltpu.VMEM((BANDS, BANDS), F32),
            pltpu.VMEM((2, 4, GROUP * BANDS, POINTS), F32),
            pltpu.SemaphoreType.DMA((4,)),
            pltpu.SemaphoreType.DMA((CELLS // GROUP,)),
        ],
        compiler_params=params(60),
        cost_estimate=cost(2 * 2048 * 512 * 3072, 8 * MIB),
        name="gradient_pass",
    )(occupancy, values, grads, cell_nodes)


def gather_kernel(wave_row_ref, slot_row_ref, came_ref, mix_ref):
    for c in range(CELLS):
        row = wave_row_ref[c]
        for f in range(3):
            place = f * CELLS + c
            mix_ref[place : place + 1, :] = came_ref[row, :, lanes(f)]
    for s in range(SLOTS):
        row = slot_row_ref[s]
        source = jnp.minimum(row, ROWS - 1)
        for q in range(RANKS):
            value = came_ref[source, :, FIELDS + q * PART : FIELDS + (q + 1) * PART]
            place = HELD + q * SLOTS + s
            mix_ref[place : place + 1, :] = jnp.where(row < ROWS, value, 0.0)


def gather(wave_rows, slot_rows, came):
    return pl.pallas_call(
        gather_kernel,
        out_shape=jax.ShapeDtypeStruct((MIX, PART), F32),
        in_specs=[SM, SM, VM],
        out_specs=VM,
        compiler_params=params(8),
        cost_estimate=cost(1e6, MIB),
        name="gather",
    )(wave_rows, slot_rows, came)


def exchange_terms(density, square):
    third = jnp.exp(jnp.log(density) * (1.0 / 3.0))
    power_four = density * third
    reduced = reduced_coef * square / (power_four * power_four)
    inner = 1.0 + slope_coef * reduced / bound_kappa
    slope = slope_coef / (inner * inner)
    enhance = 1.0 + bound_kappa - bound_kappa / inner
    d_density = -slater_coef * third * ((4.0 / 3.0) * enhance - (8.0 / 3.0) * reduced * slope)
    d_square = -slater_coef * reduced_coef * slope / power_four
    return d_density, d_square


def second_kernel(
    band_ref, m0_ref, m1_ref, m2_ref, m3_ref, a_ref, b_ref, c_ref, d_ref, val_ref, grad_ref,
    core_ref, weight_ref, shape_ref, stiff_ref, node_hbm, val_hbm, grad_hbm,
    out_hbm, rest_ref,
    field_ref, wt_ref, node_ref, table_ref, slab_ref, prod_ref, wide_ref, out_ref, source_ref, node_sem, table_sem, out_sem,
):
    groups = CELLS // GROUP
    tables = [pltpu.make_async_copy(val_hbm, table_ref.at[:, :POINTS], table_sem.at[0])]
    for k in range(3):
        tables.append(
            pltpu.make_async_copy(
                grad_hbm.at[k], table_ref.at[:, (k + 1) * POINTS : (k + 2) * POINTS], table_sem.at[k + 1]
            )
        )

    def take(g):
        rows = pl.ds(g * GROUP * BANDS, GROUP * BANDS)
        return pltpu.make_async_copy(node_hbm.at[rows], node_ref.at[rows], node_sem.at[g])

    for g in range(groups):
        take(g).start()
    for table in tables:
        table.start()
    for d, source in enumerate((m0_ref, m1_ref, m2_ref, m3_ref)):
        field_ref[(band_ref[0] + RANKS - d) & (RANKS - 1)] = source[:HELD, :]
    for q in range(RANKS):
        cols = lanes(q)
        total = [(a_ref[k, :, cols] + b_ref[k, :, cols]) + (c_ref[k, :, cols] + d_ref[k, :, cols]) for k in range(4)]
        core, weight, hartree = [field_ref[q, f * CELLS : (f + 1) * CELLS, :] for f in range(3)]
        square = total[1] * total[1] + total[2] * total[2] + total[3] * total[3]
        d_density, d_square = exchange_terms(core + total[0], square)
        wt_ref[q, :CELLS, :] = weight * (d_density + hartree)
        for k in range(1, 4):
            wt_ref[q, k * CELLS : (k + 1) * CELLS, :] = 2.0 * weight * d_square * total[k]

    def evaluate(g, k):
        rows = slice(g * GROUP * BANDS, (g + 1) * GROUP * BANDS)
        slab_ref[g % 2, k] = jnp.dot(
            node_ref[rows, :NODES], grad_ref[k - 1] if k else val_ref[...], preferred_element_type=F32
        )

    def products(g, i):
        c = g * GROUP + i
        rows = slice(i * BANDS, (i + 1) * BANDS)
        for lane in range(RANKS):
            r = [wt_ref[lane, k * CELLS + c : k * CELLS + c + 1, :] for k in range(4)]
            q = [slab_ref[g % 2, k, rows, lanes(lane)] for k in range(4)]
            value = r[0] * q[0] + (r[1] * q[1] + r[2] * q[2] + r[3] * q[3])
            prod_ref[g % 2, rows, lanes(lane)] = value.astype(BF16)
            for k in range(1, 4):
                prod_ref[g % 2, rows, lanes(4 * k + lane)] = (r[k] * q[0]).astype(BF16)

    def multiply(g, pair):
        rows = slice(2 * pair * BANDS, 2 * (pair + 1) * BANDS)
        result = lax.dot_general(
            table_ref[...], prod_ref[g % 2, rows, :], NT, preferred_element_type=F32
        )
        for i in range(2):
            c = g * GROUP + 2 * pair + i
            wide_ref[pl.ds(c, NODES, stride=CELLS), :] = result[:, i * BANDS : (i + 1) * BANDS]

    take(0).wait()
    for k in range(4):
        evaluate(0, k)
    for g in range(1, groups):
        take(g).wait()
    for table in tables:
        table.wait()
    for g in range(groups):
        for i in range(GROUP):
            if g + 1 < groups:
                evaluate(g + 1, i)
            products(g, i)
            if i % 2 == 1:
                multiply(g, i // 2)

    def leave(i):
        part = pl.ds(i * STEP, STEP)
        return pltpu.make_async_copy(out_ref.at[part], out_hbm.at[part], out_sem.at[i])

    for i in range(NODES // STEP):
        part = wide_ref[pl.ds(i * STEP * CELLS, STEP * CELLS), :].reshape(STEP, CELLS, BANDS)
        out_ref[pl.ds(i * STEP, STEP)] = part.astype(BF16)
        leave(i).start()

    for q in range(RANKS):
        rows = slice(HELD + q * SLOTS, HELD + (q + 1) * SLOTS)
        dens = (m0_ref[rows, :] + m1_ref[rows, :]) + (m2_ref[rows, :] + m3_ref[rows, :])
        source_ref[:, lanes(q)] = weight_ref[:, lanes(q)] * (core_ref[:, lanes(q)] + dens)
    drawn = lax.dot_general(source_ref[...], shape_ref[...], NT, precision=EXACT, preferred_element_type=F32)
    rest_ref[...] = stiff_ref[...] - drawn
    for i in range(NODES // STEP):
        leave(i).wait()


def second_pass(band, mixes, parts, values, grads, cell_nodes, core, weight, shape, stiff):
    return pl.pallas_call(
        second_kernel,
        out_shape=(
            jax.ShapeDtypeStruct((NODES, CELLS, BANDS), BF16),
            jax.ShapeDtypeStruct((SLOTS, ENODES), F32),
        ),
        in_specs=[SM] + [VM] * 14 + [HB] * 3,
        out_specs=(HB, VM),
        scratch_shapes=[
            pltpu.VMEM((RANKS, HELD, PART), F32),
            pltpu.VMEM((RANKS, 4 * CELLS, PART), F32),
            pltpu.VMEM((CELLS * BANDS, KPAD), BF16),
            pltpu.VMEM((NODES, 4 * POINTS), BF16),
            pltpu.VMEM((2, 4, GROUP * BANDS, POINTS), F32),
            pltpu.VMEM((2, GROUP * BANDS, 4 * POINTS), BF16),
            pltpu.VMEM((NODES * CELLS, BANDS), F32),
            pltpu.VMEM((NODES, CELLS, BANDS), BF16),
            pltpu.VMEM((SLOTS, POINTS), F32),
            pltpu.SemaphoreType.DMA((CELLS // GROUP,)),
            pltpu.SemaphoreType.DMA((4,)),
            pltpu.SemaphoreType.DMA((NODES // STEP,)),
        ],
        compiler_params=params(36),
        cost_estimate=cost(4 * 2048 * 512 * 3072, 8 * MIB),
        name="second_pass",
    )(band, *mixes, *parts, values, grads, core, weight, shape, stiff, cell_nodes, values, grads)


def stiff_kernel(nodes_ref, stiff_ref, scale_ref, out_ref):
    product = lax.dot_general(nodes_ref[...], stiff_ref[...], NT, precision=EXACT, preferred_element_type=F32)
    spread = jnp.broadcast_to(scale_ref[...], (128, SLOTS)).T
    for j in range(0, ENODES, 128):
        width = min(128, ENODES - j)
        out_ref[:, j : j + width] = product[:, j : j + width] * spread[:, :width]


def stiff_part(nodes, stiffness, scale):
    return pl.pallas_call(
        stiff_kernel,
        out_shape=jax.ShapeDtypeStruct((SLOTS, ENODES), F32),
        in_specs=[VM] * 3,
        out_specs=VM,
        compiler_params=params(12),
        cost_estimate=cost(12 * SLOTS * ENODES * ENODES, 3 * MIB),
        name="stiff_part",
    )(nodes, stiffness, scale)


def shift(array, distance):
    return lax.ppermute(array, "band", [(i, (i + distance) % RANKS) for i in range(RANKS)])


def body(
    orbitals, occupancy, shape_values, shape_grads, cell_slot, slot_cell, potential_nodes,
    stiffness, stiff_scale, electro_shape, core_density, quad_weight,
):
    values, grads = shape_values.T, shape_grads.transpose(0, 2, 1)
    nodes, shape = potential_nodes.T, electro_shape.T
    occupancy = occupancy.reshape(1, BANDS)
    band = lax.axis_index("band").astype(I32).reshape(1)

    send, cell_nodes, wave_rows, slot_rows = first_pass(
        band, slot_cell, cell_slot, orbitals, occupancy, values, nodes, shape, core_density, quad_weight
    )
    came = lax.all_to_all(send, "dom", split_axis=0, concat_axis=0, tiled=True)
    part = gradient_pass(occupancy, values, grads, cell_nodes)
    parts = [part] + [shift(part, d) for d in (1, 2, 3)]
    mix = gather(wave_rows, slot_rows, came)
    mixes = [mix] + [shift(mix, d) for d in (1, 2, 3)]
    stiff = stiff_part(nodes, stiffness, stiff_scale.reshape(1, SLOTS))
    action, rest = second_pass(
        band, mixes, parts, values, grads, cell_nodes, core_density, quad_weight, shape, stiff
    )
    return action, rest.T


def solution(mesh):
    return jax.shard_map(
        body,
        mesh=mesh,
        in_specs=(
            P(None, "dom", "band"), P("band"), P(), P(), P("dom"), P("dom"),
            P(None, "dom"), P(), P("dom"), P(), P("dom", None), P("dom", None),
        ),
        out_specs=(P(None, "dom", "band"), P(None, "dom")),
        check_vma=False,
    )
```

```python
import functools

import jax
import jax.numpy as jnp
from jax import lax
from jax.experimental import pallas as pl
from jax.experimental.pallas import tpu as pltpu
from jax.sharding import PartitionSpec as P

F32, BF16, I32 = jnp.float32, jnp.bfloat16, jnp.int32
NODES, CELLS, BANDS, POINTS = 343, 24, 128, 512
KPAD = 384
SLOTS, ENODES, DOMAINS, CAP = 48, 729, 64, 2
ROWS = DOMAINS * CAP
RANKS, PART = 4, 128
GROUP = 4
STEP = 49
FIELDS = 3 * PART
WIDTH = FIELDS + POINTS
TERMS = 4 * CELLS
MIX = TERMS + RANKS * SLOTS
EXACT = lax.Precision.HIGH
NT = (((1,), (1,)), ((), ()))
MIB = 1 << 20

slater_coef = 0.7385587663820224
bound_kappa = 0.804
slope_coef = 0.2195149727645171
reduced_coef = 0.026121172985233605

VM = pl.BlockSpec(memory_space=pltpu.VMEM)
SM = pl.BlockSpec(memory_space=pltpu.SMEM)
HB = pl.BlockSpec(memory_space=pltpu.HBM)


def params(mib):
    return pltpu.CompilerParams(vmem_limit_bytes=mib * MIB)


def cost(flops, nbytes):
    return pl.CostEstimate(flops=int(flops), bytes_accessed=int(nbytes), transcendentals=0)


def lanes(index):
    return slice(index * 128, index * 128 + 128)


def first_kernel(
    band_ref, slot_cell_ref, cell_slot_ref,
    orb_hbm, occ_ref, val_hbm, nodes_hbm, shape_hbm, core_hbm, weight_hbm,
    send_hbm, node_hbm, wave_row_ref, slot_row_ref,
    orb_ref, val_ref, nodes_ref, shape_ref, field_ref, send_ref,
    wide_ref, node_ref, table_ref, spread_ref, sum_ref, count_ref, in_sem, orb_sem, out_sem, send_sem,
):
    mine = pl.ds(pl.multiple_of(band_ref[0] * PART, PART), PART)
    chunks = NODES // STEP

    def take(i):
        part = pl.ds(i * STEP, STEP)
        return pltpu.make_async_copy(orb_hbm.at[part], orb_ref.at[part], orb_sem.at[i])

    loads = [
        pltpu.make_async_copy(val_hbm, val_ref, in_sem.at[0]),
        pltpu.make_async_copy(nodes_hbm, nodes_ref, in_sem.at[1]),
        pltpu.make_async_copy(shape_hbm.at[:, mine], shape_ref, in_sem.at[2]),
        pltpu.make_async_copy(core_hbm.at[:, mine], field_ref.at[:, lanes(0)], in_sem.at[3]),
        pltpu.make_async_copy(weight_hbm.at[:, mine], field_ref.at[:, lanes(1)], in_sem.at[4]),
    ]
    for load in loads:
        load.start()
    for i in range(chunks):
        take(i).start()

    for d in range(DOMAINS + 1):
        count_ref[d] = 0
    for s in range(SLOTS):
        cell = slot_cell_ref[s]
        filled = cell >= 0
        source = jnp.where(filled, lax.shift_right_logical(cell * 10923, 18), DOMAINS)
        place = jnp.minimum(count_ref[source], CAP - 1)
        count_ref[source] = jnp.where(filled, place + 1, 0)
        slot_row_ref[s] = jnp.where(filled, source * CAP + place, ROWS)
    for d in range(DOMAINS):
        count_ref[d] = -1
    for c in range(CELLS):
        slot = cell_slot_ref[c]
        owner = lax.shift_right_logical(slot * 21846, 20)
        other = count_ref[owner]
        known = other >= 0
        first = jnp.maximum(other, 0)
        later = known & (cell_slot_ref[first] > slot)
        wave_row_ref[c] = owner * CAP + jnp.where(known & jnp.logical_not(later), 1, 0)
        target = jnp.where(later, first, c)
        wave_row_ref[target] = jnp.where(later, owner * CAP + 1, wave_row_ref[c])
        count_ref[owner] = c

    spread_ref[...] = jnp.broadcast_to(occ_ref[...], (BANDS, BANDS)).T
    table_ref[NODES - 7 :, :] = jnp.zeros((KPAD - NODES + 7, POINTS), BF16)
    wide_ref[NODES * CELLS :, :] = jnp.zeros(((KPAD - NODES) * CELLS, BANDS), F32)

    for load in loads:
        load.wait()
    table_ref[:NODES, :] = val_ref[...]
    field_ref[:, lanes(2)] = jnp.dot(
        nodes_ref[...], shape_ref[...], precision=EXACT, preferred_element_type=F32
    )
    for s in range(SLOTS):
        send_ref[slot_row_ref[s], :, :FIELDS] = field_ref[s : s + 1, :]

    for i in range(chunks):
        take(i).wait()
        part = orb_ref[pl.ds(i * STEP, STEP)].astype(F32)
        wide_ref[pl.ds(i * STEP * CELLS, STEP * CELLS), :] = part.reshape(STEP * CELLS, BANDS)

    def store(g):
        rows = pl.ds(g * GROUP * BANDS, GROUP * BANDS)
        return pltpu.make_async_copy(node_ref.at[rows], node_hbm.at[rows], out_sem.at[g])

    groups = CELLS // GROUP
    for g in range(groups):
        rows = slice(g * GROUP * BANDS, (g + 1) * GROUP * BANDS)
        for i in range(GROUP):
            c = g * GROUP + i
            block = wide_ref[pl.ds(c, KPAD, stride=CELLS), :]
            node_ref[c * BANDS : (c + 1) * BANDS, :] = block.T.astype(BF16)
        store(g).start()
        values = jnp.dot(node_ref[rows, :], table_ref[...], preferred_element_type=F32)
        for i in range(GROUP):
            c = g * GROUP + i
            for q in range(RANKS):
                lead = values[i * BANDS : (i + 1) * BANDS, lanes(q)]
                sum_ref[c : c + 1, lanes(q)] = jnp.sum(spread_ref[...] * lead * lead, axis=0, keepdims=True)
    for c in range(CELLS):
        send_ref[wave_row_ref[c], :, FIELDS:] = sum_ref[c : c + 1, :]
    leave = pltpu.make_async_copy(send_ref.at[pl.ds(0, ROWS)], send_hbm, send_sem)
    leave.start()
    for g in range(groups):
        store(g).wait()
    leave.wait()


def first_pass(band, slot_cell, cell_slot, orbitals, occupancy, values, nodes, shape, core, weight):
    return pl.pallas_call(
        first_kernel,
        out_shape=(
            jax.ShapeDtypeStruct((ROWS, 1, WIDTH), F32),
            jax.ShapeDtypeStruct((CELLS * BANDS, KPAD), BF16),
            jax.ShapeDtypeStruct((CELLS,), I32),
            jax.ShapeDtypeStruct((SLOTS,), I32),
        ),
        in_specs=[SM, SM, SM, HB, VM] + [HB] * 5,
        out_specs=(HB, HB, SM, SM),
        scratch_shapes=[
            pltpu.VMEM((NODES, CELLS, BANDS), BF16),
            pltpu.VMEM((NODES, POINTS), BF16),
            pltpu.VMEM((SLOTS, ENODES), F32),
            pltpu.VMEM((ENODES, PART), F32),
            pltpu.VMEM((SLOTS, FIELDS), F32),
            pltpu.VMEM((ROWS + 1, 1, WIDTH), F32),
            pltpu.VMEM((KPAD * CELLS, BANDS), F32),
            pltpu.VMEM((CELLS * BANDS, KPAD), BF16),
            pltpu.VMEM((KPAD, POINTS), BF16),
            pltpu.VMEM((BANDS, BANDS), F32),
            pltpu.VMEM((CELLS, POINTS), F32),
            pltpu.SMEM((DOMAINS + 1,), I32),
            pltpu.SemaphoreType.DMA((5,)),
            pltpu.SemaphoreType.DMA((NODES // STEP,)),
            pltpu.SemaphoreType.DMA((CELLS // GROUP,)),
            pltpu.SemaphoreType.DMA,
        ],
        compiler_params=params(60),
        cost_estimate=cost(2 * 512 * 512 * 3072, 8 * MIB),
        name="first_pass",
    )(band, slot_cell, cell_slot, orbitals, occupancy, values, nodes, shape, core, weight)


def gradient_kernel(
    band_ref, occ_ref, val_hbm, grad_hbm, node_hbm,
    part0_ref, part1_ref, part2_ref, part3_ref,
    table_ref, node_ref, spread_ref, slab_ref, sum_ref, table_sem, node_sem,
):
    groups = CELLS // GROUP

    def take(g):
        rows = pl.ds(g * GROUP * BANDS, GROUP * BANDS)
        return pltpu.make_async_copy(node_hbm.at[rows], node_ref.at[rows], node_sem.at[g])

    tables = [pltpu.make_async_copy(val_hbm, table_ref.at[0], table_sem.at[0])]
    for k in range(3):
        tables.append(pltpu.make_async_copy(grad_hbm.at[k], table_ref.at[k + 1], table_sem.at[k + 1]))
    tables[0].start()
    take(0).start()
    for k in range(1, 4):
        tables[k].start()
    for g in range(1, groups):
        take(g).start()
    spread_ref[...] = jnp.broadcast_to(occ_ref[...], (BANDS, BANDS)).T
    take(0).wait()

    def evaluate(g, k):
        rows = slice(g * GROUP * BANDS, (g + 1) * GROUP * BANDS)
        slab_ref[g % 2, k] = jnp.dot(node_ref[rows, :NODES], table_ref[k], preferred_element_type=F32)

    def reduce(g, i):
        c = g * GROUP + i
        bands = slice(i * BANDS, (i + 1) * BANDS)
        for q in range(RANKS):
            lead = slab_ref[g % 2, 0, bands, lanes(q)]
            scaled = spread_ref[...] * lead
            sum_ref[q, 0, c : c + 1, :] = jnp.sum(scaled * lead, axis=0, keepdims=True)
            for k in range(1, 4):
                term = slab_ref[g % 2, k, bands, lanes(q)]
                sum_ref[q, k, c : c + 1, :] = 2.0 * jnp.sum(scaled * term, axis=0, keepdims=True)

    for k in range(4):
        tables[k].wait()
        evaluate(0, k)
    for g in range(1, groups):
        take(g).wait()
    for g in range(groups):
        for i in range(GROUP):
            if g + 1 < groups:
                evaluate(g + 1, i)
            reduce(g, i)
    for d, part_ref in enumerate((part0_ref, part1_ref, part2_ref, part3_ref)):
        part_ref[...] = sum_ref[(band_ref[0] + d) & (RANKS - 1)]


def gradient_pass(band, occupancy, values, grads, cell_nodes):
    part = jax.ShapeDtypeStruct((4, CELLS, PART), F32)
    return pl.pallas_call(
        gradient_kernel,
        out_shape=(part, part, part, part),
        in_specs=[SM, VM] + [HB] * 3,
        out_specs=(VM, VM, VM, VM),
        scratch_shapes=[
            pltpu.VMEM((4, NODES, POINTS), BF16),
            pltpu.VMEM((CELLS * BANDS, KPAD), BF16),
            pltpu.VMEM((BANDS, BANDS), F32),
            pltpu.VMEM((2, 4, GROUP * BANDS, POINTS), F32),
            pltpu.VMEM((RANKS, 4, CELLS, PART), F32),
            pltpu.SemaphoreType.DMA((4,)),
            pltpu.SemaphoreType.DMA((CELLS // GROUP,)),
        ],
        compiler_params=params(60),
        cost_estimate=cost(2 * 2048 * 512 * 3072, 8 * MIB),
        name="gradient_pass",
    )(band, occupancy, values, grads, cell_nodes)


def exchange_terms(density, square):
    third = jnp.exp(jnp.log(density) * (1.0 / 3.0))
    power_four = density * third
    reduced = reduced_coef * square / (power_four * power_four)
    inner = 1.0 + slope_coef * reduced / bound_kappa
    slope = slope_coef / (inner * inner)
    enhance = 1.0 + bound_kappa - bound_kappa / inner
    d_density = -slater_coef * third * ((4.0 / 3.0) * enhance - (8.0 / 3.0) * reduced * slope)
    d_square = -slater_coef * reduced_coef * slope / power_four
    return d_density, d_square


def gather_kernel(wave_row_ref, slot_row_ref, came_ref, part_ref, field_ref, dens_ref, own_ref):
    own_ref[...] = part_ref[...]
    for c in range(CELLS):
        row = wave_row_ref[c]
        for f in range(3):
            place = f * CELLS + c
            field_ref[place : place + 1, :] = came_ref[row, :, lanes(f)]
    for s in range(SLOTS):
        row = slot_row_ref[s]
        source = jnp.minimum(row, ROWS - 1)
        for q in range(RANKS):
            value = came_ref[source, :, FIELDS + q * PART : FIELDS + (q + 1) * PART]
            place = q * SLOTS + s
            dens_ref[place : place + 1, :] = jnp.where(row < ROWS, value, 0.0)


def gather(wave_rows, slot_rows, came, part):
    return pl.pallas_call(
        gather_kernel,
        out_shape=(
            jax.ShapeDtypeStruct((3 * CELLS, PART), F32),
            jax.ShapeDtypeStruct((RANKS * SLOTS, PART), F32),
            jax.ShapeDtypeStruct((4, CELLS, PART), F32),
        ),
        in_specs=[SM, SM, VM, VM],
        out_specs=(VM, VM, VM),
        compiler_params=params(8),
        cost_estimate=cost(1e6, MIB),
        name="gather",
    )(wave_rows, slot_rows, came, part)


def exchange_kernel(field_ref, dens_ref, a_ref, b_ref, c_ref, d_ref, mix_ref):
    total = [(a_ref[k] + b_ref[k]) + (c_ref[k] + d_ref[k]) for k in range(4)]
    core, weight, hartree = [field_ref[f * CELLS : (f + 1) * CELLS, :] for f in range(3)]
    square = total[1] * total[1] + total[2] * total[2] + total[3] * total[3]
    d_density, d_square = exchange_terms(core + total[0], square)
    mix_ref[:CELLS, :] = weight * (d_density + hartree)
    for k in range(1, 4):
        mix_ref[k * CELLS : (k + 1) * CELLS, :] = 2.0 * weight * d_square * total[k]
    mix_ref[TERMS:, :] = dens_ref[...]


def exchange(field, dens, parts):
    return pl.pallas_call(
        exchange_kernel,
        out_shape=jax.ShapeDtypeStruct((MIX, PART), F32),
        in_specs=[VM] * 6,
        out_specs=VM,
        compiler_params=params(8),
        cost_estimate=cost(1e6, MIB),
        name="exchange",
    )(field, dens, *parts)


def second_kernel(
    band_ref, m0_ref, m1_ref, m2_ref, m3_ref, val_ref, grad_ref,
    core_ref, weight_ref, shape_ref, stiff_ref, node_hbm, val_hbm, grad_hbm,
    out_hbm, rest_ref,
    wt_ref, node_ref, table_ref, slab_ref, prod_ref, wide_ref, out_ref, source_ref, node_sem, table_sem, out_sem,
):
    groups = CELLS // GROUP
    tables = [pltpu.make_async_copy(val_hbm, table_ref.at[:, :POINTS], table_sem.at[0])]
    for k in range(3):
        tables.append(
            pltpu.make_async_copy(
                grad_hbm.at[k], table_ref.at[:, (k + 1) * POINTS : (k + 2) * POINTS], table_sem.at[k + 1]
            )
        )

    def take(g):
        rows = pl.ds(g * GROUP * BANDS, GROUP * BANDS)
        return pltpu.make_async_copy(node_hbm.at[rows], node_ref.at[rows], node_sem.at[g])

    for g in range(groups):
        take(g).start()
    for table in tables:
        table.start()
    for d, source in enumerate((m0_ref, m1_ref, m2_ref, m3_ref)):
        wt_ref[(band_ref[0] + RANKS - d) & (RANKS - 1)] = source[:TERMS, :]

    def evaluate(g, k):
        rows = slice(g * GROUP * BANDS, (g + 1) * GROUP * BANDS)
        slab_ref[g % 2, k] = jnp.dot(
            node_ref[rows, :NODES], grad_ref[k - 1] if k else val_ref[...], preferred_element_type=F32
        )

    def products(g, i):
        c = g * GROUP + i
        rows = slice(i * BANDS, (i + 1) * BANDS)
        for lane in range(RANKS):
            r = [wt_ref[lane, k * CELLS + c : k * CELLS + c + 1, :] for k in range(4)]
            q = [slab_ref[g % 2, k, rows, lanes(lane)] for k in range(4)]
            value = r[0] * q[0] + (r[1] * q[1] + r[2] * q[2] + r[3] * q[3])
            prod_ref[g % 2, rows, lanes(lane)] = value.astype(BF16)
            for k in range(1, 4):
                prod_ref[g % 2, rows, lanes(4 * k + lane)] = (r[k] * q[0]).astype(BF16)

    def multiply(g, pair):
        rows = slice(2 * pair * BANDS, 2 * (pair + 1) * BANDS)
        result = lax.dot_general(
            table_ref[...], prod_ref[g % 2, rows, :], NT, preferred_element_type=F32
        )
        for i in range(2):
            c = g * GROUP + 2 * pair + i
            wide_ref[pl.ds(c, NODES, stride=CELLS), :] = result[:, i * BANDS : (i + 1) * BANDS]

    take(0).wait()
    for k in range(4):
        evaluate(0, k)
    for g in range(1, groups):
        take(g).wait()
    for table in tables:
        table.wait()
    for g in range(groups):
        for i in range(GROUP):
            if g + 1 < groups:
                evaluate(g + 1, i)
            products(g, i)
            if i % 2 == 1:
                multiply(g, i // 2)

    def leave(i):
        part = pl.ds(i * STEP, STEP)
        return pltpu.make_async_copy(out_ref.at[part], out_hbm.at[part], out_sem.at[i])

    for i in range(NODES // STEP):
        part = wide_ref[pl.ds(i * STEP * CELLS, STEP * CELLS), :].reshape(STEP, CELLS, BANDS)
        out_ref[pl.ds(i * STEP, STEP)] = part.astype(BF16)
        leave(i).start()

    for q in range(RANKS):
        rows = slice(TERMS + q * SLOTS, TERMS + (q + 1) * SLOTS)
        dens = (m0_ref[rows, :] + m1_ref[rows, :]) + (m2_ref[rows, :] + m3_ref[rows, :])
        source_ref[:, lanes(q)] = weight_ref[:, lanes(q)] * (core_ref[:, lanes(q)] + dens)
    drawn = lax.dot_general(source_ref[...], shape_ref[...], NT, precision=EXACT, preferred_element_type=F32)
    rest_ref[...] = stiff_ref[...] - drawn
    for i in range(NODES // STEP):
        leave(i).wait()


def second_pass(band, mixes, values, grads, cell_nodes, core, weight, shape, stiff):
    cell_nodes = pltpu.with_memory_space_constraint(cell_nodes, pltpu.HBM)
    return pl.pallas_call(
        second_kernel,
        out_shape=(
            jax.ShapeDtypeStruct((NODES, CELLS, BANDS), BF16),
            jax.ShapeDtypeStruct((SLOTS, ENODES), F32),
        ),
        in_specs=[SM] + [VM] * 10 + [HB] * 3,
        out_specs=(HB, VM),
        scratch_shapes=[
            pltpu.VMEM((RANKS, TERMS, PART), F32),
            pltpu.VMEM((CELLS * BANDS, KPAD), BF16),
            pltpu.VMEM((NODES, 4 * POINTS), BF16),
            pltpu.VMEM((2, 4, GROUP * BANDS, POINTS), F32),
            pltpu.VMEM((2, GROUP * BANDS, 4 * POINTS), BF16),
            pltpu.VMEM((NODES * CELLS, BANDS), F32),
            pltpu.VMEM((NODES, CELLS, BANDS), BF16),
            pltpu.VMEM((SLOTS, POINTS), F32),
            pltpu.SemaphoreType.DMA((CELLS // GROUP,)),
            pltpu.SemaphoreType.DMA((4,)),
            pltpu.SemaphoreType.DMA((NODES // STEP,)),
        ],
        compiler_params=params(36),
        cost_estimate=cost(4 * 2048 * 512 * 3072, 8 * MIB),
        name="second_pass",
    )(band, *mixes, values, grads, core, weight, shape, stiff, cell_nodes, values, grads)


def stiff_kernel(nodes_ref, stiff_ref, scale_ref, out_ref):
    product = lax.dot_general(nodes_ref[...], stiff_ref[...], NT, precision=EXACT, preferred_element_type=F32)
    spread = jnp.broadcast_to(scale_ref[...], (128, SLOTS)).T
    for j in range(0, ENODES, 128):
        width = min(128, ENODES - j)
        out_ref[:, j : j + width] = product[:, j : j + width] * spread[:, :width]


def stiff_part(nodes, stiffness, scale):
    return pl.pallas_call(
        stiff_kernel,
        out_shape=jax.ShapeDtypeStruct((SLOTS, ENODES), F32),
        in_specs=[VM] * 3,
        out_specs=VM,
        compiler_params=params(12),
        cost_estimate=cost(12 * SLOTS * ENODES * ENODES, 3 * MIB),
        name="stiff_part",
    )(nodes, stiffness, scale)


def shift(array, distance):
    return lax.ppermute(array, "band", [(i, (i + distance) % RANKS) for i in range(RANKS)])


def body(
    orbitals, occupancy, shape_values, shape_grads, cell_slot, slot_cell, potential_nodes,
    stiffness, stiff_scale, electro_shape, core_density, quad_weight,
):
    values, grads = shape_values.T, shape_grads.transpose(0, 2, 1)
    nodes, shape = potential_nodes.T, electro_shape.T
    occupancy = occupancy.reshape(1, BANDS)
    band = lax.axis_index("band").astype(I32).reshape(1)

    send, cell_nodes, wave_rows, slot_rows = first_pass(
        band, slot_cell, cell_slot, orbitals, occupancy, values, nodes, shape, core_density, quad_weight
    )
    came = lax.all_to_all(send, "dom", split_axis=0, concat_axis=0, tiled=True)
    parts = gradient_pass(band, occupancy, values, grads, cell_nodes)
    others = [shift(parts[d], d) for d in (1, 2, 3)]
    stiff = stiff_part(nodes, stiffness, stiff_scale.reshape(1, SLOTS))
    field, dens, own = gather(wave_rows, slot_rows, came, parts[0])
    mix = exchange(field, dens, [own] + others)
    mixes = [mix] + [shift(mix, d) for d in (1, 2, 3)]
    action, rest = second_pass(
        band, mixes, values, grads, cell_nodes, core_density, quad_weight, shape, stiff
    )
    return action, rest.T


def solution(mesh):
    return jax.shard_map(
        body,
        mesh=mesh,
        in_specs=(
            P(None, "dom", "band"), P("band"), P(), P(), P("dom"), P("dom"),
            P(None, "dom"), P(), P("dom"), P(), P("dom", None), P("dom", None),
        ),
        out_specs=(P(None, "dom", "band"), P(None, "dom")),
        check_vma=False,
    )
```

```python
import functools

import jax
import jax.numpy as jnp
from jax import lax
from jax.experimental import pallas as pl
from jax.experimental.pallas import tpu as pltpu
from jax.sharding import PartitionSpec as P

F32, BF16, I32 = jnp.float32, jnp.bfloat16, jnp.int32
NODES, CELLS, BANDS, POINTS = 343, 24, 128, 512
KPAD = 384
SLOTS, ENODES, DOMAINS, CAP = 48, 729, 64, 2
ROWS = DOMAINS * CAP
RANKS, PART = 4, 128
GROUP = 4
STEP = 49
FIELDS = 3 * PART
WIDTH = FIELDS + POINTS
TERMS = 4 * CELLS
MIX = TERMS + RANKS * SLOTS
EXACT = lax.Precision.HIGH
NT = (((1,), (1,)), ((), ()))
MIB = 1 << 20

slater_coef = 0.7385587663820224
bound_kappa = 0.804
slope_coef = 0.2195149727645171
reduced_coef = 0.026121172985233605

VM = pl.BlockSpec(memory_space=pltpu.VMEM)
SM = pl.BlockSpec(memory_space=pltpu.SMEM)
HB = pl.BlockSpec(memory_space=pltpu.HBM)


def params(mib):
    return pltpu.CompilerParams(vmem_limit_bytes=mib * MIB)


def cost(flops, nbytes):
    return pl.CostEstimate(flops=int(flops), bytes_accessed=int(nbytes), transcendentals=0)


def lanes(index):
    return slice(index * 128, index * 128 + 128)


def first_kernel(
    band_ref, slot_cell_ref, cell_slot_ref,
    orb_hbm, occ_ref, val_hbm, nodes_hbm, shape_hbm, core_hbm, weight_hbm,
    send_hbm, node_hbm, head_hbm, wave_row_ref, slot_row_ref,
    orb_ref, val_ref, nodes_ref, shape_ref, field_ref, send_ref,
    wide_ref, node_ref, table_ref, spread_ref, sum_ref, count_ref, in_sem, orb_sem, out_sem, send_sem, head_sem,
):
    mine = pl.ds(pl.multiple_of(band_ref[0] * PART, PART), PART)
    chunks = NODES // STEP

    def take(i):
        part = pl.ds(i * STEP, STEP)
        return pltpu.make_async_copy(orb_hbm.at[part], orb_ref.at[part], orb_sem.at[i])

    loads = [
        pltpu.make_async_copy(val_hbm, val_ref, in_sem.at[0]),
        pltpu.make_async_copy(nodes_hbm, nodes_ref, in_sem.at[1]),
        pltpu.make_async_copy(shape_hbm.at[:, mine], shape_ref, in_sem.at[2]),
        pltpu.make_async_copy(core_hbm.at[:, mine], field_ref.at[:, lanes(0)], in_sem.at[3]),
        pltpu.make_async_copy(weight_hbm.at[:, mine], field_ref.at[:, lanes(1)], in_sem.at[4]),
    ]
    for load in loads:
        load.start()
    for i in range(chunks):
        take(i).start()

    for d in range(DOMAINS + 1):
        count_ref[d] = 0
    for s in range(SLOTS):
        cell = slot_cell_ref[s]
        filled = cell >= 0
        source = jnp.where(filled, lax.shift_right_logical(cell * 10923, 18), DOMAINS)
        place = jnp.minimum(count_ref[source], CAP - 1)
        count_ref[source] = jnp.where(filled, place + 1, 0)
        slot_row_ref[s] = jnp.where(filled, source * CAP + place, ROWS)
    for d in range(DOMAINS):
        count_ref[d] = -1
    for c in range(CELLS):
        slot = cell_slot_ref[c]
        owner = lax.shift_right_logical(slot * 21846, 20)
        other = count_ref[owner]
        known = other >= 0
        first = jnp.maximum(other, 0)
        later = known & (cell_slot_ref[first] > slot)
        wave_row_ref[c] = owner * CAP + jnp.where(known & jnp.logical_not(later), 1, 0)
        target = jnp.where(later, first, c)
        wave_row_ref[target] = jnp.where(later, owner * CAP + 1, wave_row_ref[c])
        count_ref[owner] = c

    spread_ref[...] = jnp.broadcast_to(occ_ref[...], (BANDS, BANDS)).T
    table_ref[NODES - 7 :, :] = jnp.zeros((KPAD - NODES + 7, POINTS), BF16)
    wide_ref[NODES * CELLS :, :] = jnp.zeros(((KPAD - NODES) * CELLS, BANDS), F32)

    for load in loads:
        load.wait()
    table_ref[:NODES, :] = val_ref[...]
    field_ref[:, lanes(2)] = jnp.dot(
        nodes_ref[...], shape_ref[...], precision=EXACT, preferred_element_type=F32
    )
    for s in range(SLOTS):
        send_ref[slot_row_ref[s], :, :FIELDS] = field_ref[s : s + 1, :]

    for i in range(chunks):
        take(i).wait()
        part = orb_ref[pl.ds(i * STEP, STEP)].astype(F32)
        wide_ref[pl.ds(i * STEP * CELLS, STEP * CELLS), :] = part.reshape(STEP * CELLS, BANDS)

    def store(g):
        rows = pl.ds(g * GROUP * BANDS, GROUP * BANDS)
        return pltpu.make_async_copy(node_ref.at[rows], node_hbm.at[rows], out_sem.at[g])

    groups = CELLS // GROUP
    for g in range(groups):
        rows = slice(g * GROUP * BANDS, (g + 1) * GROUP * BANDS)
        for i in range(GROUP):
            c = g * GROUP + i
            block = wide_ref[pl.ds(c, KPAD, stride=CELLS), :]
            node_ref[c * BANDS : (c + 1) * BANDS, :] = block.T.astype(BF16)
        store(g).start()
        if g == 0:
            head = pltpu.make_async_copy(node_ref.at[pl.ds(0, GROUP * BANDS)], head_hbm, head_sem)
            head.start()
        values = jnp.dot(node_ref[rows, :], table_ref[...], preferred_element_type=F32)
        for i in range(GROUP):
            c = g * GROUP + i
            for q in range(RANKS):
                lead = values[i * BANDS : (i + 1) * BANDS, lanes(q)]
                sum_ref[c : c + 1, lanes(q)] = jnp.sum(spread_ref[...] * lead * lead, axis=0, keepdims=True)
    for c in range(CELLS):
        send_ref[wave_row_ref[c], :, FIELDS:] = sum_ref[c : c + 1, :]
    leave = pltpu.make_async_copy(send_ref.at[pl.ds(0, ROWS)], send_hbm, send_sem)
    leave.start()
    for g in range(groups):
        store(g).wait()
    head.wait()
    leave.wait()


def first_pass(band, slot_cell, cell_slot, orbitals, occupancy, values, nodes, shape, core, weight):
    return pl.pallas_call(
        first_kernel,
        out_shape=(
            jax.ShapeDtypeStruct((ROWS, 1, WIDTH), F32),
            jax.ShapeDtypeStruct((CELLS * BANDS, KPAD), BF16),
            jax.ShapeDtypeStruct((GROUP * BANDS, KPAD), BF16),
            jax.ShapeDtypeStruct((CELLS,), I32),
            jax.ShapeDtypeStruct((SLOTS,), I32),
        ),
        in_specs=[SM, SM, SM, HB, VM] + [HB] * 5,
        out_specs=(HB, HB, HB, SM, SM),
        scratch_shapes=[
            pltpu.VMEM((NODES, CELLS, BANDS), BF16),
            pltpu.VMEM((NODES, POINTS), BF16),
            pltpu.VMEM((SLOTS, ENODES), F32),
            pltpu.VMEM((ENODES, PART), F32),
            pltpu.VMEM((SLOTS, FIELDS), F32),
            pltpu.VMEM((ROWS + 1, 1, WIDTH), F32),
            pltpu.VMEM((KPAD * CELLS, BANDS), F32),
            pltpu.VMEM((CELLS * BANDS, KPAD), BF16),
            pltpu.VMEM((KPAD, POINTS), BF16),
            pltpu.VMEM((BANDS, BANDS), F32),
            pltpu.VMEM((CELLS, POINTS), F32),
            pltpu.SMEM((DOMAINS + 1,), I32),
            pltpu.SemaphoreType.DMA((5,)),
            pltpu.SemaphoreType.DMA((NODES // STEP,)),
            pltpu.SemaphoreType.DMA((CELLS // GROUP,)),
            pltpu.SemaphoreType.DMA,
            pltpu.SemaphoreType.DMA,
        ],
        compiler_params=params(60),
        cost_estimate=cost(2 * 512 * 512 * 3072, 8 * MIB),
        name="first_pass",
    )(band, slot_cell, cell_slot, orbitals, occupancy, values, nodes, shape, core, weight)


def gradient_kernel(
    band_ref, occ_ref, val_hbm, grad_hbm, node_hbm,
    part0_ref, part1_ref, part2_ref, part3_ref,
    table_ref, node_ref, spread_ref, slab_ref, sum_ref, table_sem, node_sem,
):
    groups = CELLS // GROUP

    def take(g):
        rows = pl.ds(g * GROUP * BANDS, GROUP * BANDS)
        return pltpu.make_async_copy(node_hbm.at[rows], node_ref.at[rows], node_sem.at[g])

    tables = [pltpu.make_async_copy(val_hbm, table_ref.at[0], table_sem.at[0])]
    for k in range(3):
        tables.append(pltpu.make_async_copy(grad_hbm.at[k], table_ref.at[k + 1], table_sem.at[k + 1]))
    tables[0].start()
    take(0).start()
    for k in range(1, 4):
        tables[k].start()
    for g in range(1, groups):
        take(g).start()
    spread_ref[...] = jnp.broadcast_to(occ_ref[...], (BANDS, BANDS)).T
    take(0).wait()

    for g in range(groups):
        slab = slab_ref.at[g % 2]
        rows = slice(g * GROUP * BANDS, (g + 1) * GROUP * BANDS)
        if g == 1:
            for later in range(1, groups):
                take(later).wait()
        for k in range(4):
            if g == 0:
                tables[k].wait()
            slab[k] = jnp.dot(node_ref[rows, :NODES], table_ref[k], preferred_element_type=F32)
        for i in range(GROUP):
            c = g * GROUP + i
            bands = slice(i * BANDS, (i + 1) * BANDS)
            for q in range(RANKS):
                lead = slab[0, bands, lanes(q)]
                scaled = spread_ref[...] * lead
                sum_ref[q, 0, c : c + 1, :] = jnp.sum(scaled * lead, axis=0, keepdims=True)
                for k in range(1, 4):
                    term = slab[k, bands, lanes(q)]
                    sum_ref[q, k, c : c + 1, :] = 2.0 * jnp.sum(scaled * term, axis=0, keepdims=True)
    for d, part_ref in enumerate((part0_ref, part1_ref, part2_ref, part3_ref)):
        part_ref[...] = sum_ref[(band_ref[0] + d) & (RANKS - 1)]


def gradient_pass(band, occupancy, values, grads, cell_nodes):
    part = jax.ShapeDtypeStruct((4, CELLS, PART), F32)
    return pl.pallas_call(
        gradient_kernel,
        out_shape=(part, part, part, part),
        in_specs=[SM, VM] + [HB] * 3,
        out_specs=(VM, VM, VM, VM),
        scratch_shapes=[
            pltpu.VMEM((4, NODES, POINTS), BF16),
            pltpu.VMEM((CELLS * BANDS, KPAD), BF16),
            pltpu.VMEM((BANDS, BANDS), F32),
            pltpu.VMEM((2, 4, GROUP * BANDS, POINTS), F32),
            pltpu.VMEM((RANKS, 4, CELLS, PART), F32),
            pltpu.SemaphoreType.DMA((4,)),
            pltpu.SemaphoreType.DMA((CELLS // GROUP,)),
        ],
        compiler_params=params(60),
        cost_estimate=cost(2 * 2048 * 512 * 3072, 8 * MIB),
        name="gradient_pass",
    )(band, occupancy, values, grads, cell_nodes)


def exchange_terms(density, square):
    third = jnp.exp(jnp.log(density) * (1.0 / 3.0))
    power_four = density * third
    reduced = reduced_coef * square / (power_four * power_four)
    inner = 1.0 + slope_coef * reduced / bound_kappa
    slope = slope_coef / (inner * inner)
    enhance = 1.0 + bound_kappa - bound_kappa / inner
    d_density = -slater_coef * third * ((4.0 / 3.0) * enhance - (8.0 / 3.0) * reduced * slope)
    d_square = -slater_coef * reduced_coef * slope / power_four
    return d_density, d_square


def gather_kernel(wave_row_ref, slot_row_ref, came_ref, part_ref, field_ref, dens_ref, own_ref):
    own_ref[...] = part_ref[...]
    for c in range(CELLS):
        row = wave_row_ref[c]
        for f in range(3):
            place = f * CELLS + c
            field_ref[place : place + 1, :] = came_ref[row, :, lanes(f)]
    for s in range(SLOTS):
        row = slot_row_ref[s]
        source = jnp.minimum(row, ROWS - 1)
        for q in range(RANKS):
            value = came_ref[source, :, FIELDS + q * PART : FIELDS + (q + 1) * PART]
            place = q * SLOTS + s
            dens_ref[place : place + 1, :] = jnp.where(row < ROWS, value, 0.0)


def gather(wave_rows, slot_rows, came, part):
    return pl.pallas_call(
        gather_kernel,
        out_shape=(
            jax.ShapeDtypeStruct((3 * CELLS, PART), F32),
            jax.ShapeDtypeStruct((RANKS * SLOTS, PART), F32),
            jax.ShapeDtypeStruct((4, CELLS, PART), F32),
        ),
        in_specs=[SM, SM, VM, VM],
        out_specs=(VM, VM, VM),
        compiler_params=params(8),
        cost_estimate=cost(1e6, MIB),
        name="gather",
    )(wave_rows, slot_rows, came, part)


def exchange_kernel(field_ref, dens_ref, a_ref, b_ref, c_ref, d_ref, mix_ref):
    total = [(a_ref[k] + b_ref[k]) + (c_ref[k] + d_ref[k]) for k in range(4)]
    core, weight, hartree = [field_ref[f * CELLS : (f + 1) * CELLS, :] for f in range(3)]
    square = total[1] * total[1] + total[2] * total[2] + total[3] * total[3]
    d_density, d_square = exchange_terms(core + total[0], square)
    mix_ref[:CELLS, :] = weight * (d_density + hartree)
    for k in range(1, 4):
        mix_ref[k * CELLS : (k + 1) * CELLS, :] = 2.0 * weight * d_square * total[k]
    mix_ref[TERMS:, :] = dens_ref[...]


def exchange(field, dens, parts):
    return pl.pallas_call(
        exchange_kernel,
        out_shape=jax.ShapeDtypeStruct((MIX, PART), F32),
        in_specs=[VM] * 6,
        out_specs=VM,
        compiler_params=params(8),
        cost_estimate=cost(1e6, MIB),
        name="exchange",
    )(field, dens, *parts)


def second_kernel(
    band_ref, m0_ref, m1_ref, m2_ref, m3_ref, val_ref, grad_ref, head_ref,
    core_ref, weight_ref, shape_ref, stiff_ref, node_hbm, val_hbm, grad_hbm,
    out_hbm, rest_ref,
    wt_ref, node_ref, table_ref, slab_ref, prod_ref, wide_ref, out_ref, source_ref, node_sem, table_sem, out_sem,
):
    groups = CELLS // GROUP
    tables = [pltpu.make_async_copy(val_hbm, table_ref.at[:, :POINTS], table_sem.at[0])]
    for k in range(3):
        tables.append(
            pltpu.make_async_copy(
                grad_hbm.at[k], table_ref.at[:, (k + 1) * POINTS : (k + 2) * POINTS], table_sem.at[k + 1]
            )
        )

    def take(g):
        rows = pl.ds(g * GROUP * BANDS, GROUP * BANDS)
        return pltpu.make_async_copy(node_hbm.at[rows], node_ref.at[rows], node_sem.at[g])

    for g in range(1, groups):
        take(g).start()
    for table in tables:
        table.start()
    for d, source in enumerate((m0_ref, m1_ref, m2_ref, m3_ref)):
        wt_ref[(band_ref[0] + RANKS - d) & (RANKS - 1)] = source[:TERMS, :]

    def evaluate(g, k):
        rows = slice(g * GROUP * BANDS, (g + 1) * GROUP * BANDS)
        slab_ref[g % 2, k] = jnp.dot(
            node_ref[rows, :NODES] if g else head_ref[:, :NODES],
            grad_ref[k - 1] if k else val_ref[...],
            preferred_element_type=F32,
        )

    def products(g, i):
        c = g * GROUP + i
        rows = slice(i * BANDS, (i + 1) * BANDS)
        for lane in range(RANKS):
            r = [wt_ref[lane, k * CELLS + c : k * CELLS + c + 1, :] for k in range(4)]
            q = [slab_ref[g % 2, k, rows, lanes(lane)] for k in range(4)]
            value = r[0] * q[0] + (r[1] * q[1] + r[2] * q[2] + r[3] * q[3])
            prod_ref[g % 2, rows, lanes(lane)] = value.astype(BF16)
            for k in range(1, 4):
                prod_ref[g % 2, rows, lanes(4 * k + lane)] = (r[k] * q[0]).astype(BF16)

    def multiply(g, pair):
        rows = slice(2 * pair * BANDS, 2 * (pair + 1) * BANDS)
        result = lax.dot_general(
            table_ref[...], prod_ref[g % 2, rows, :], NT, preferred_element_type=F32
        )
        for i in range(2):
            c = g * GROUP + 2 * pair + i
            wide_ref[pl.ds(c, NODES, stride=CELLS), :] = result[:, i * BANDS : (i + 1) * BANDS]

    for k in range(4):
        evaluate(0, k)
    for g in range(1, groups):
        take(g).wait()
    for table in tables:
        table.wait()
    for g in range(groups):
        for i in range(GROUP):
            if g + 1 < groups:
                evaluate(g + 1, i)
            products(g, i)
            if i % 2 == 1:
                multiply(g, i // 2)

    def leave(i):
        part = pl.ds(i * STEP, STEP)
        return pltpu.make_async_copy(out_ref.at[part], out_hbm.at[part], out_sem.at[i])

    for i in range(NODES // STEP):
        part = wide_ref[pl.ds(i * STEP * CELLS, STEP * CELLS), :].reshape(STEP, CELLS, BANDS)
        out_ref[pl.ds(i * STEP, STEP)] = part.astype(BF16)
        leave(i).start()

    for q in range(RANKS):
        rows = slice(TERMS + q * SLOTS, TERMS + (q + 1) * SLOTS)
        dens = (m0_ref[rows, :] + m1_ref[rows, :]) + (m2_ref[rows, :] + m3_ref[rows, :])
        source_ref[:, lanes(q)] = weight_ref[:, lanes(q)] * (core_ref[:, lanes(q)] + dens)
    drawn = lax.dot_general(source_ref[...], shape_ref[...], NT, precision=EXACT, preferred_element_type=F32)
    rest_ref[...] = stiff_ref[...] - drawn
    for i in range(NODES // STEP):
        leave(i).wait()


def second_pass(band, mixes, values, grads, head, cell_nodes, core, weight, shape, stiff):
    cell_nodes = pltpu.with_memory_space_constraint(cell_nodes, pltpu.HBM)
    return pl.pallas_call(
        second_kernel,
        out_shape=(
            jax.ShapeDtypeStruct((NODES, CELLS, BANDS), BF16),
            jax.ShapeDtypeStruct((SLOTS, ENODES), F32),
        ),
        in_specs=[SM] + [VM] * 11 + [HB] * 3,
        out_specs=(HB, VM),
        scratch_shapes=[
            pltpu.VMEM((RANKS, TERMS, PART), F32),
            pltpu.VMEM((CELLS * BANDS, KPAD), BF16),
            pltpu.VMEM((NODES, 4 * POINTS), BF16),
            pltpu.VMEM((2, 4, GROUP * BANDS, POINTS), F32),
            pltpu.VMEM((2, GROUP * BANDS, 4 * POINTS), BF16),
            pltpu.VMEM((NODES * CELLS, BANDS), F32),
            pltpu.VMEM((NODES, CELLS, BANDS), BF16),
            pltpu.VMEM((SLOTS, POINTS), F32),
            pltpu.SemaphoreType.DMA((CELLS // GROUP,)),
            pltpu.SemaphoreType.DMA((4,)),
            pltpu.SemaphoreType.DMA((NODES // STEP,)),
        ],
        compiler_params=params(36),
        cost_estimate=cost(4 * 2048 * 512 * 3072, 8 * MIB),
        name="second_pass",
    )(band, *mixes, values, grads, head, core, weight, shape, stiff, cell_nodes, values, grads)


def stiff_kernel(nodes_ref, stiff_ref, scale_ref, out_ref):
    product = lax.dot_general(nodes_ref[...], stiff_ref[...], NT, precision=EXACT, preferred_element_type=F32)
    spread = jnp.broadcast_to(scale_ref[...], (128, SLOTS)).T
    for j in range(0, ENODES, 128):
        width = min(128, ENODES - j)
        out_ref[:, j : j + width] = product[:, j : j + width] * spread[:, :width]


def stiff_part(nodes, stiffness, scale):
    return pl.pallas_call(
        stiff_kernel,
        out_shape=jax.ShapeDtypeStruct((SLOTS, ENODES), F32),
        in_specs=[VM] * 3,
        out_specs=VM,
        compiler_params=params(12),
        cost_estimate=cost(12 * SLOTS * ENODES * ENODES, 3 * MIB),
        name="stiff_part",
    )(nodes, stiffness, scale)


def shift(array, distance):
    return lax.ppermute(array, "band", [(i, (i + distance) % RANKS) for i in range(RANKS)])


def body(
    orbitals, occupancy, shape_values, shape_grads, cell_slot, slot_cell, potential_nodes,
    stiffness, stiff_scale, electro_shape, core_density, quad_weight,
):
    values, grads = shape_values.T, shape_grads.transpose(0, 2, 1)
    nodes, shape = potential_nodes.T, electro_shape.T
    occupancy = occupancy.reshape(1, BANDS)
    band = lax.axis_index("band").astype(I32).reshape(1)

    send, cell_nodes, head, wave_rows, slot_rows = first_pass(
        band, slot_cell, cell_slot, orbitals, occupancy, values, nodes, shape, core_density, quad_weight
    )
    came = lax.all_to_all(send, "dom", split_axis=0, concat_axis=0, tiled=True)
    parts = gradient_pass(band, occupancy, values, grads, cell_nodes)
    others = [shift(parts[d], d) for d in (1, 2, 3)]
    stiff = stiff_part(nodes, stiffness, stiff_scale.reshape(1, SLOTS))
    field, dens, own = gather(wave_rows, slot_rows, came, parts[0])
    mix = exchange(field, dens, [own] + others)
    mixes = [mix] + [shift(mix, d) for d in (1, 2, 3)]
    action, rest = second_pass(
        band, mixes, values, grads, head, cell_nodes, core_density, quad_weight, shape, stiff
    )
    return action, rest.T


def solution(mesh):
    return jax.shard_map(
        body,
        mesh=mesh,
        in_specs=(
            P(None, "dom", "band"), P("band"), P(), P(), P("dom"), P("dom"),
            P(None, "dom"), P(), P("dom"), P(), P("dom", None), P("dom", None),
        ),
        out_specs=(P(None, "dom", "band"), P(None, "dom")),
        check_vma=False,
    )
```

```python
import functools

import jax
import jax.numpy as jnp
from jax import lax
from jax.experimental import pallas as pl
from jax.experimental.pallas import tpu as pltpu
from jax.sharding import PartitionSpec as P

F32, BF16, I32 = jnp.float32, jnp.bfloat16, jnp.int32
NODES, CELLS, BANDS, POINTS = 343, 24, 128, 512
KPAD = 384
SLOTS, ENODES, DOMAINS, CAP = 48, 729, 64, 2
ROWS = DOMAINS * CAP
RANKS, PART = 4, 128
GROUP = 4
STEP = 49
FIELDS = 3 * PART
WIDTH = FIELDS + POINTS
TERMS = 4 * CELLS
MIX = TERMS + RANKS * SLOTS
EXACT = lax.Precision.HIGH
NT = (((1,), (1,)), ((), ()))
MIB = 1 << 20

slater_coef = 0.7385587663820224
bound_kappa = 0.804
slope_coef = 0.2195149727645171
reduced_coef = 0.026121172985233605

VM = pl.BlockSpec(memory_space=pltpu.VMEM)
SM = pl.BlockSpec(memory_space=pltpu.SMEM)
HB = pl.BlockSpec(memory_space=pltpu.HBM)


def params(mib):
    return pltpu.CompilerParams(vmem_limit_bytes=mib * MIB)


def cost(flops, nbytes):
    return pl.CostEstimate(flops=int(flops), bytes_accessed=int(nbytes), transcendentals=0)


def lanes(index):
    return slice(index * 128, index * 128 + 128)


def first_kernel(
    band_ref, slot_cell_ref, cell_slot_ref,
    orb_hbm, occ_ref, val_hbm, nodes_hbm, shape_hbm, core_hbm, weight_hbm,
    send_hbm, node_hbm, head_hbm, wave_row_ref, slot_row_ref,
    orb_ref, val_ref, nodes_ref, shape_ref, field_ref, send_ref,
    wide_ref, node_ref, table_ref, spread_ref, sum_ref, count_ref, in_sem, orb_sem, out_sem, send_sem, head_sem,
):
    mine = pl.ds(pl.multiple_of(band_ref[0] * PART, PART), PART)
    chunks = NODES // STEP

    def take(i):
        part = pl.ds(i * STEP, STEP)
        return pltpu.make_async_copy(orb_hbm.at[part], orb_ref.at[part], orb_sem.at[i])

    loads = [
        pltpu.make_async_copy(val_hbm, val_ref, in_sem.at[0]),
        pltpu.make_async_copy(nodes_hbm, nodes_ref, in_sem.at[1]),
        pltpu.make_async_copy(shape_hbm.at[:, mine], shape_ref, in_sem.at[2]),
        pltpu.make_async_copy(core_hbm.at[:, mine], field_ref.at[:, lanes(0)], in_sem.at[3]),
        pltpu.make_async_copy(weight_hbm.at[:, mine], field_ref.at[:, lanes(1)], in_sem.at[4]),
    ]
    for load in loads:
        load.start()
    for i in range(chunks):
        take(i).start()

    for d in range(DOMAINS + 1):
        count_ref[d] = 0
    for s in range(SLOTS):
        cell = slot_cell_ref[s]
        filled = cell >= 0
        source = jnp.where(filled, lax.shift_right_logical(cell * 10923, 18), DOMAINS)
        place = jnp.minimum(count_ref[source], CAP - 1)
        count_ref[source] = jnp.where(filled, place + 1, 0)
        slot_row_ref[s] = jnp.where(filled, source * CAP + place, ROWS)
    for d in range(DOMAINS):
        count_ref[d] = -1
    for c in range(CELLS):
        slot = cell_slot_ref[c]
        owner = lax.shift_right_logical(slot * 21846, 20)
        other = count_ref[owner]
        known = other >= 0
        first = jnp.maximum(other, 0)
        later = known & (cell_slot_ref[first] > slot)
        wave_row_ref[c] = owner * CAP + jnp.where(known & jnp.logical_not(later), 1, 0)
        target = jnp.where(later, first, c)
        wave_row_ref[target] = jnp.where(later, owner * CAP + 1, wave_row_ref[c])
        count_ref[owner] = c

    spread_ref[...] = jnp.broadcast_to(occ_ref[...], (BANDS, BANDS)).T
    table_ref[NODES - 7 :, :] = jnp.zeros((KPAD - NODES + 7, POINTS), BF16)
    wide_ref[NODES * CELLS :, :] = jnp.zeros(((KPAD - NODES) * CELLS, BANDS), F32)

    for load in loads:
        load.wait()
    table_ref[:NODES, :] = val_ref[...]
    field_ref[:, lanes(2)] = jnp.dot(
        nodes_ref[...], shape_ref[...], precision=EXACT, preferred_element_type=F32
    )
    for s in range(SLOTS):
        send_ref[slot_row_ref[s], :, :FIELDS] = field_ref[s : s + 1, :]

    for i in range(chunks):
        take(i).wait()
        part = orb_ref[pl.ds(i * STEP, STEP)].astype(F32)
        wide_ref[pl.ds(i * STEP * CELLS, STEP * CELLS), :] = part.reshape(STEP * CELLS, BANDS)

    def store(g):
        rows = pl.ds(g * GROUP * BANDS, GROUP * BANDS)
        return pltpu.make_async_copy(node_ref.at[rows], node_hbm.at[rows], out_sem.at[g])

    groups = CELLS // GROUP
    for g in range(groups):
        rows = slice(g * GROUP * BANDS, (g + 1) * GROUP * BANDS)
        for i in range(GROUP):
            c = g * GROUP + i
            block = wide_ref[pl.ds(c, KPAD, stride=CELLS), :]
            node_ref[c * BANDS : (c + 1) * BANDS, :] = block.T.astype(BF16)
        store(g).start()
        if g == 0:
            head = pltpu.make_async_copy(node_ref.at[pl.ds(0, GROUP * BANDS)], head_hbm, head_sem)
            head.start()
        values = jnp.dot(node_ref[rows, :], table_ref[...], preferred_element_type=F32)
        for i in range(GROUP):
            c = g * GROUP + i
            for q in range(RANKS):
                lead = values[i * BANDS : (i + 1) * BANDS, lanes(q)]
                sum_ref[c : c + 1, lanes(q)] = jnp.sum(spread_ref[...] * lead * lead, axis=0, keepdims=True)
    for c in range(CELLS):
        send_ref[wave_row_ref[c], :, FIELDS:] = sum_ref[c : c + 1, :]
    leave = pltpu.make_async_copy(send_ref.at[pl.ds(0, ROWS)], send_hbm, send_sem)
    leave.start()
    for g in range(groups):
        store(g).wait()
    head.wait()
    leave.wait()


def first_pass(band, slot_cell, cell_slot, orbitals, occupancy, values, nodes, shape, core, weight):
    return pl.pallas_call(
        first_kernel,
        out_shape=(
            jax.ShapeDtypeStruct((ROWS, 1, WIDTH), F32),
            jax.ShapeDtypeStruct((CELLS * BANDS, KPAD), BF16),
            jax.ShapeDtypeStruct((GROUP * BANDS, KPAD), BF16),
            jax.ShapeDtypeStruct((CELLS,), I32),
            jax.ShapeDtypeStruct((SLOTS,), I32),
        ),
        in_specs=[SM, SM, SM, HB, VM] + [HB] * 5,
        out_specs=(HB, HB, HB, SM, SM),
        scratch_shapes=[
            pltpu.VMEM((NODES, CELLS, BANDS), BF16),
            pltpu.VMEM((NODES, POINTS), BF16),
            pltpu.VMEM((SLOTS, ENODES), F32),
            pltpu.VMEM((ENODES, PART), F32),
            pltpu.VMEM((SLOTS, FIELDS), F32),
            pltpu.VMEM((ROWS + 1, 1, WIDTH), F32),
            pltpu.VMEM((KPAD * CELLS, BANDS), F32),
            pltpu.VMEM((CELLS * BANDS, KPAD), BF16),
            pltpu.VMEM((KPAD, POINTS), BF16),
            pltpu.VMEM((BANDS, BANDS), F32),
            pltpu.VMEM((CELLS, POINTS), F32),
            pltpu.SMEM((DOMAINS + 1,), I32),
            pltpu.SemaphoreType.DMA((5,)),
            pltpu.SemaphoreType.DMA((NODES // STEP,)),
            pltpu.SemaphoreType.DMA((CELLS // GROUP,)),
            pltpu.SemaphoreType.DMA,
            pltpu.SemaphoreType.DMA,
        ],
        compiler_params=params(60),
        cost_estimate=cost(2 * 512 * 512 * 3072, 8 * MIB),
        name="first_pass",
    )(band, slot_cell, cell_slot, orbitals, occupancy, values, nodes, shape, core, weight)


def gradient_kernel(
    band_ref, occ_ref, val_hbm, grad_hbm, node_hbm,
    part0_ref, part1_ref, part2_ref, part3_ref,
    table_ref, node_ref, spread_ref, slab_ref, sum_ref, table_sem, node_sem,
):
    groups = CELLS // GROUP

    def take(g):
        rows = pl.ds(g * GROUP * BANDS, GROUP * BANDS)
        return pltpu.make_async_copy(node_hbm.at[rows], node_ref.at[rows], node_sem.at[g])

    tables = [pltpu.make_async_copy(val_hbm, table_ref.at[0], table_sem.at[0])]
    for k in range(3):
        tables.append(pltpu.make_async_copy(grad_hbm.at[k], table_ref.at[k + 1], table_sem.at[k + 1]))
    tables[0].start()
    take(0).start()
    for k in range(1, 4):
        tables[k].start()
    for g in range(1, groups):
        take(g).start()
    spread_ref[...] = jnp.broadcast_to(occ_ref[...], (BANDS, BANDS)).T
    take(0).wait()

    for g in range(groups):
        slab = slab_ref.at[g % 2]
        rows = slice(g * GROUP * BANDS, (g + 1) * GROUP * BANDS)
        if g == 1:
            for later in range(1, groups):
                take(later).wait()
        for k in range(4):
            if g == 0:
                tables[k].wait()
            slab[k] = jnp.dot(node_ref[rows, :NODES], table_ref[k], preferred_element_type=F32)
        for i in range(GROUP):
            c = g * GROUP + i
            bands = slice(i * BANDS, (i + 1) * BANDS)
            for q in range(RANKS):
                lead = slab[0, bands, lanes(q)]
                scaled = spread_ref[...] * lead
                sum_ref[q, 0, c : c + 1, :] = jnp.sum(scaled * lead, axis=0, keepdims=True)
                for k in range(1, 4):
                    term = slab[k, bands, lanes(q)]
                    sum_ref[q, k, c : c + 1, :] = 2.0 * jnp.sum(scaled * term, axis=0, keepdims=True)
    for d, part_ref in enumerate((part0_ref, part1_ref, part2_ref, part3_ref)):
        part_ref[...] = sum_ref[(band_ref[0] + d) & (RANKS - 1)]


def gradient_pass(band, occupancy, values, grads, cell_nodes):
    part = jax.ShapeDtypeStruct((4, CELLS, PART), F32)
    return pl.pallas_call(
        gradient_kernel,
        out_shape=(part, part, part, part),
        in_specs=[SM, VM] + [HB] * 3,
        out_specs=(VM, VM, VM, VM),
        scratch_shapes=[
            pltpu.VMEM((4, NODES, POINTS), BF16),
            pltpu.VMEM((CELLS * BANDS, KPAD), BF16),
            pltpu.VMEM((BANDS, BANDS), F32),
            pltpu.VMEM((2, 4, GROUP * BANDS, POINTS), F32),
            pltpu.VMEM((RANKS, 4, CELLS, PART), F32),
            pltpu.SemaphoreType.DMA((4,)),
            pltpu.SemaphoreType.DMA((CELLS // GROUP,)),
        ],
        compiler_params=params(60),
        cost_estimate=cost(2 * 2048 * 512 * 3072, 8 * MIB),
        name="gradient_pass",
    )(band, occupancy, values, grads, cell_nodes)


def exchange_terms(density, square):
    third = jnp.exp(jnp.log(density) * (1.0 / 3.0))
    power_four = density * third
    reduced = reduced_coef * square / (power_four * power_four)
    inner = 1.0 + slope_coef * reduced / bound_kappa
    slope = slope_coef / (inner * inner)
    enhance = 1.0 + bound_kappa - bound_kappa / inner
    d_density = -slater_coef * third * ((4.0 / 3.0) * enhance - (8.0 / 3.0) * reduced * slope)
    d_square = -slater_coef * reduced_coef * slope / power_four
    return d_density, d_square


def gather_kernel(wave_row_ref, slot_row_ref, came_ref, part_ref, field_ref, dens_ref, own_ref):
    own_ref[...] = part_ref[...]
    for c in range(CELLS):
        row = wave_row_ref[c]
        for f in range(3):
            place = f * CELLS + c
            field_ref[place : place + 1, :] = came_ref[row, :, lanes(f)]
    for s in range(SLOTS):
        row = slot_row_ref[s]
        source = jnp.minimum(row, ROWS - 1)
        for q in range(RANKS):
            value = came_ref[source, :, FIELDS + q * PART : FIELDS + (q + 1) * PART]
            place = q * SLOTS + s
            dens_ref[place : place + 1, :] = jnp.where(row < ROWS, value, 0.0)


def gather(wave_rows, slot_rows, came, part):
    return pl.pallas_call(
        gather_kernel,
        out_shape=(
            jax.ShapeDtypeStruct((3 * CELLS, PART), F32),
            jax.ShapeDtypeStruct((RANKS * SLOTS, PART), F32),
            jax.ShapeDtypeStruct((4, CELLS, PART), F32),
        ),
        in_specs=[SM, SM, VM, VM],
        out_specs=(VM, VM, VM),
        compiler_params=params(8),
        cost_estimate=cost(1e6, MIB),
        name="gather",
    )(wave_rows, slot_rows, came, part)


def exchange_kernel(field_ref, dens_ref, a_ref, b_ref, c_ref, d_ref, mix_ref):
    total = [(a_ref[k] + b_ref[k]) + (c_ref[k] + d_ref[k]) for k in range(4)]
    core, weight, hartree = [field_ref[f * CELLS : (f + 1) * CELLS, :] for f in range(3)]
    square = total[1] * total[1] + total[2] * total[2] + total[3] * total[3]
    d_density, d_square = exchange_terms(core + total[0], square)
    mix_ref[:CELLS, :] = weight * (d_density + hartree)
    for k in range(1, 4):
        mix_ref[k * CELLS : (k + 1) * CELLS, :] = 2.0 * weight * d_square * total[k]
    mix_ref[TERMS:, :] = dens_ref[...]


def exchange(field, dens, parts):
    return pl.pallas_call(
        exchange_kernel,
        out_shape=jax.ShapeDtypeStruct((MIX, PART), F32),
        in_specs=[VM] * 6,
        out_specs=VM,
        compiler_params=params(8),
        cost_estimate=cost(1e6, MIB),
        name="exchange",
    )(field, dens, *parts)


def second_kernel(
    band_ref, m0_ref, m1_ref, m2_ref, m3_ref, val_ref, grad_ref, head_ref,
    core_ref, weight_ref, shape_ref, stiff_ref, node_hbm, val_hbm, grad_hbm,
    out_hbm, rest_ref,
    wt_ref, node_ref, table_ref, slab_ref, prod_ref, wide_ref, out_ref, source_ref, node_sem, table_sem, out_sem,
):
    groups = CELLS // GROUP
    tables = [pltpu.make_async_copy(val_hbm, table_ref.at[:, :POINTS], table_sem.at[0])]
    for k in range(3):
        tables.append(
            pltpu.make_async_copy(
                grad_hbm.at[k], table_ref.at[:, (k + 1) * POINTS : (k + 2) * POINTS], table_sem.at[k + 1]
            )
        )

    def take(g):
        rows = pl.ds(g * GROUP * BANDS, GROUP * BANDS)
        return pltpu.make_async_copy(node_hbm.at[rows], node_ref.at[rows], node_sem.at[g])

    for g in range(1, groups):
        take(g).start()
    for table in tables:
        table.start()
    for d, source in enumerate((m0_ref, m1_ref, m2_ref, m3_ref)):
        wt_ref[(band_ref[0] + RANKS - d) & (RANKS - 1)] = source[:TERMS, :]

    def evaluate(g, k):
        rows = slice(g * GROUP * BANDS, (g + 1) * GROUP * BANDS)
        slab_ref[g % 2, k] = jnp.dot(
            node_ref[rows, :NODES] if g else head_ref[:, :NODES],
            grad_ref[k - 1] if k else val_ref[...],
            preferred_element_type=F32,
        )

    def products(g, i):
        c = g * GROUP + i
        rows = slice(i * BANDS, (i + 1) * BANDS)
        for lane in range(RANKS):
            r = [wt_ref[lane, k * CELLS + c : k * CELLS + c + 1, :] for k in range(4)]
            q = [slab_ref[g % 2, k, rows, lanes(lane)] for k in range(4)]
            value = r[0] * q[0] + (r[1] * q[1] + r[2] * q[2] + r[3] * q[3])
            prod_ref[g % 2, rows, lanes(lane)] = value.astype(BF16)
            for k in range(1, 4):
                prod_ref[g % 2, rows, lanes(4 * k + lane)] = (r[k] * q[0]).astype(BF16)

    def multiply(g, pair):
        rows = slice(2 * pair * BANDS, 2 * (pair + 1) * BANDS)
        result = lax.dot_general(
            table_ref[...], prod_ref[g % 2, rows, :], NT, preferred_element_type=F32
        )
        for i in range(2):
            c = g * GROUP + 2 * pair + i
            wide_ref[pl.ds(c, NODES, stride=CELLS), :] = result[:, i * BANDS : (i + 1) * BANDS]

    for k in range(4):
        evaluate(0, k)
    for g in range(1, groups):
        take(g).wait()
    for table in tables:
        table.wait()
    for g in range(groups):
        for i in range(GROUP):
            if g + 1 < groups:
                evaluate(g + 1, i)
            products(g, i)
            if i % 2 == 1:
                multiply(g, i // 2)

    def leave(i):
        part = pl.ds(i * STEP, STEP)
        return pltpu.make_async_copy(out_ref.at[part], out_hbm.at[part], out_sem.at[i])

    for i in range(NODES // STEP):
        part = wide_ref[pl.ds(i * STEP * CELLS, STEP * CELLS), :].reshape(STEP, CELLS, BANDS)
        out_ref[pl.ds(i * STEP, STEP)] = part.astype(BF16)
        leave(i).start()

    for q in range(RANKS):
        rows = slice(TERMS + q * SLOTS, TERMS + (q + 1) * SLOTS)
        dens = (m0_ref[rows, :] + m1_ref[rows, :]) + (m2_ref[rows, :] + m3_ref[rows, :])
        source_ref[:, lanes(q)] = weight_ref[:, lanes(q)] * (core_ref[:, lanes(q)] + dens)
    drawn = lax.dot_general(source_ref[...], shape_ref[...], NT, precision=EXACT, preferred_element_type=F32)
    rest_ref[...] = stiff_ref[...] - drawn
    for i in range(NODES // STEP):
        leave(i).wait()


def second_pass(band, mixes, values, grads, head, cell_nodes, core, weight, shape, stiff):
    cell_nodes = pltpu.with_memory_space_constraint(cell_nodes, pltpu.HBM)
    return pl.pallas_call(
        second_kernel,
        out_shape=(
            jax.ShapeDtypeStruct((NODES, CELLS, BANDS), BF16),
            jax.ShapeDtypeStruct((SLOTS, ENODES), F32),
        ),
        in_specs=[SM] + [VM] * 11 + [HB] * 3,
        out_specs=(HB, VM),
        scratch_shapes=[
            pltpu.VMEM((RANKS, TERMS, PART), F32),
            pltpu.VMEM((CELLS * BANDS, KPAD), BF16),
            pltpu.VMEM((NODES, 4 * POINTS), BF16),
            pltpu.VMEM((2, 4, GROUP * BANDS, POINTS), F32),
            pltpu.VMEM((2, GROUP * BANDS, 4 * POINTS), BF16),
            pltpu.VMEM(((NODES + 1) * CELLS, BANDS), F32),
            pltpu.VMEM((NODES, CELLS, BANDS), BF16),
            pltpu.VMEM((SLOTS, POINTS), F32),
            pltpu.SemaphoreType.DMA((CELLS // GROUP,)),
            pltpu.SemaphoreType.DMA((4,)),
            pltpu.SemaphoreType.DMA((NODES // STEP,)),
        ],
        compiler_params=params(36),
        cost_estimate=cost(4 * 2048 * 512 * 3072, 8 * MIB),
        name="second_pass",
    )(band, *mixes, values, grads, head, core, weight, shape, stiff, cell_nodes, values, grads)


def stiff_kernel(nodes_ref, stiff_ref, scale_ref, out_ref):
    product = lax.dot_general(nodes_ref[...], stiff_ref[...], NT, precision=EXACT, preferred_element_type=F32)
    spread = jnp.broadcast_to(scale_ref[...], (128, SLOTS)).T
    for j in range(0, ENODES, 128):
        width = min(128, ENODES - j)
        out_ref[:, j : j + width] = product[:, j : j + width] * spread[:, :width]


def stiff_part(nodes, stiffness, scale):
    return pl.pallas_call(
        stiff_kernel,
        out_shape=jax.ShapeDtypeStruct((SLOTS, ENODES), F32),
        in_specs=[VM] * 3,
        out_specs=VM,
        compiler_params=params(12),
        cost_estimate=cost(12 * SLOTS * ENODES * ENODES, 3 * MIB),
        name="stiff_part",
    )(nodes, stiffness, scale)


def shift(array, distance):
    return lax.ppermute(array, "band", [(i, (i + distance) % RANKS) for i in range(RANKS)])


def body(
    orbitals, occupancy, shape_values, shape_grads, cell_slot, slot_cell, potential_nodes,
    stiffness, stiff_scale, electro_shape, core_density, quad_weight,
):
    values, grads = shape_values.T, shape_grads.transpose(0, 2, 1)
    nodes, shape = potential_nodes.T, electro_shape.T
    occupancy = occupancy.reshape(1, BANDS)
    band = lax.axis_index("band").astype(I32).reshape(1)

    send, cell_nodes, head, wave_rows, slot_rows = first_pass(
        band, slot_cell, cell_slot, orbitals, occupancy, values, nodes, shape, core_density, quad_weight
    )
    came = lax.all_to_all(send, "dom", split_axis=0, concat_axis=0, tiled=True)
    parts = gradient_pass(band, occupancy, values, grads, cell_nodes)
    others = [shift(parts[d], d) for d in (1, 2, 3)]
    stiff = stiff_part(nodes, stiffness, stiff_scale.reshape(1, SLOTS))
    field, dens, own = gather(wave_rows, slot_rows, came, parts[0])
    mix = exchange(field, dens, [own] + others)
    mixes = [mix] + [shift(mix, d) for d in (1, 2, 3)]
    action, rest = second_pass(
        band, mixes, values, grads, head, cell_nodes, core_density, quad_weight, shape, stiff
    )
    return action, rest.T


def solution(mesh):
    return jax.shard_map(
        body,
        mesh=mesh,
        in_specs=(
            P(None, "dom", "band"), P("band"), P(), P(), P("dom"), P("dom"),
            P(None, "dom"), P(), P("dom"), P(), P("dom", None), P("dom", None),
        ),
        out_specs=(P(None, "dom", "band"), P(None, "dom")),
        check_vma=False,
    )
```
